256 devices in a mesh: det: 32 (over z, y), sky: 8 (over x, core).
Axes of the slice: x: 4, y: 4, z: 8, core: 2. Of those that a mesh axis runs over, the one named last changes fastest.
Arguments:
- timelines: float32 [1024, 32768], P(('det', 'sky')), may hold values from -18 to 18
- knee_freq: float32 [1024], P(('det', 'sky')), may hold values from 1 to 100
- noise_slope: float32 [1024], P(('det', 'sky')), may hold values from 1 to 4
- noise_level: float32 [1024], P(('det', 'sky')), may hold values from 0.5 to 2
- templates: float32 [1024, 512], replicated, as said below
- interval_bounds: int32 [33], replicated, may hold values from 0 to 32768, as said below
- block_index: int32 [1024, 256], replicated, may hold values from 0 to 255
- block_slot: int32 [256], replicated, may hold values from 0 to 255, each once
Outputs:
- owned_map: float32 [256, 128], P('sky')
The draws below stay inside these ranges and needn't reach their ends.
Inputs may be any that keep to these rules, and one draw needn't show every extreme that they name: interval_bounds starts at 0, ends at 32768 and rises strictly through multiples of 128; no interval is longer than 2048 samples, and in every draw one is exactly 2048 long. The columns of templates are orthonormal. Each row number appears once; sky index block_slot[b] // 32 owns block b.
All inputs are finite; a program needn't handle non-finite values.
Results may differ from the reference program's by a relative error of at most 0.000092.
Values sent between devices are 32-bit elements; how exact they have to be, the bound alone decides.
No kernel may reach another device: no remote copies, remote signals or barrier semaphores. Data moves between devices by JAX's collectives and lax.ppermute only.
A program may use at most 64 MiB of HBM per device.

```python
import math
import jax
import jax.numpy as jnp
from jax import lax

DETS = 1024
SAMPLES = 32768
TEMPLATES = 512
SEGLEN = 128
BLOCKS = 256
INTERVALS = 32
SEGMENTS = 256
LONGEST = 2048
MEANHITS = 1024


def draw_timelines(key, part):
    noise_key = jax.random.fold_in(key, 101)
    level_key = jax.random.fold_in(key, 102)
    base_noise = jnp.clip(jax.random.normal(noise_key, (DETS, SAMPLES), jnp.float32), -6.0, 6.0)
    levels = jnp.exp(jax.random.uniform(level_key, (DETS, SEGMENTS), jnp.float32, math.log(0.3), math.log(3.0)))
    return base_noise * jnp.repeat(levels, SEGLEN, axis=1)


def draw_templates(key, part):
    row_order = jax.random.permutation(jax.random.fold_in(key, 201), DETS)
    column_pick = jax.random.permutation(jax.random.fold_in(key, 202), DETS)[:TEMPLATES]
    row_sign = 1 - 2 * jax.random.randint(jax.random.fold_in(key, 203), (DETS,), 0, 2)
    column_sign = 1 - 2 * jax.random.randint(jax.random.fold_in(key, 204), (TEMPLATES,), 0, 2)
    intersection = jnp.bitwise_and(row_order[:, None], column_pick[None, :])
    parity = jnp.zeros_like(intersection)
    for bit_pos in range(DETS.bit_length()):
        parity = parity + jnp.bitwise_and(jnp.right_shift(intersection, bit_pos), 1)
    signs = (1 - 2 * (parity % 2)) * row_sign[:, None] * column_sign[None, :]
    return signs.astype(jnp.float32) * (1.0 / math.sqrt(DETS))


def draw_interval_bounds(key, part):
    unit_total = SAMPLES // SEGLEN
    interval_count = INTERVALS
    mean_units = unit_total // interval_count
    share_cut = mean_units // (interval_count - 1)
    extra_cut = mean_units % (interval_count - 1)
    lowest_base = mean_units - share_cut - (1 if extra_cut > 0 else 0)
    role_order = jax.random.permutation(jax.random.fold_in(key, 301), interval_count)
    other_rank = role_order - 1
    base_units = mean_units - share_cut - (other_rank < extra_cut).astype(jnp.int32)
    offsets = jax.random.randint(jax.random.fold_in(key, 302), (interval_count,), 0, lowest_base)
    pair_shift = jnp.take(offsets, jnp.maximum(other_rank, 0) // 2)
    paired = (other_rank % 2 == 1) | (other_rank + 1 <= interval_count - 2)
    direction = jnp.where(other_rank % 2 == 0, 1, -1)
    lengths = jnp.where(role_order == 0, 2 * mean_units, base_units + jnp.where(paired, direction * pair_shift, 0))
    ends = jnp.cumsum(lengths * SEGLEN).astype(jnp.int32)
    return jnp.concatenate([jnp.zeros((1,), jnp.int32), ends])


def with_ends(values, key, smallest, high):
    extent = values.shape
    spot = [jax.random.randint(jax.random.fold_in(key, axis), (), 0, extent[axis]) for axis in range(len(extent))]
    values = values.at[tuple(spot)].set(smallest)
    longest = extent.index(max(extent))
    spot[longest] = (spot[longest] + 1) % extent[longest]
    return values.at[tuple(spot)].set(high)


def block_scale(rng, dims, split, least, high):
    level = 1.0
    for axis_at, shards_of in split:
        draws = jax.random.uniform(jax.random.fold_in(jax.random.fold_in(rng, 6), axis_at), (shards_of,), jnp.float32, least / len(split), high / len(split))
        level = level * jnp.repeat(jnp.exp(draws), dims[axis_at] // shards_of).reshape((-1,) + (1,) * (len(dims) - 1 - axis_at))
    return level


def setup_inputs(seed: int = 0) -> dict:
    keys = jax.random.split(jax.random.key(seed), 9)
    return {
        "timelines": draw_timelines(jax.random.fold_in(keys[8], 71), 0),
        "knee_freq": jnp.clip(jnp.exp(math.log(100.0) - 4.6051702 * jax.random.uniform(keys[1], (DETS,), jnp.float32) ** block_scale(keys[1], (DETS,), ((0, 256),), -0.2, 0.2)), 1.0, 100.0),
        "noise_slope": jnp.clip(jnp.exp(math.log(4.0) - 1.3862944 * jax.random.uniform(keys[2], (DETS,), jnp.float32) ** block_scale(keys[2], (DETS,), ((0, 256),), -0.2, 0.2)), 1.0, 4.0),
        "noise_level": jnp.clip(jnp.exp(math.log(2.0) - 1.3862944 * jax.random.uniform(keys[3], (DETS,), jnp.float32) ** block_scale(keys[3], (DETS,), ((0, 256),), -0.2, 0.2)), 0.5, 2.0),
        "templates": draw_templates(jax.random.fold_in(keys[8], 71), 0),
        "interval_bounds": draw_interval_bounds(jax.random.fold_in(keys[8], 71), 0),
        "block_index": with_ends(jax.random.randint(keys[6], (DETS, SEGMENTS), 0, BLOCKS), jax.random.fold_in(keys[6], 1), 0, BLOCKS - 1).astype(jnp.int32),
        "block_slot": jax.random.permutation(keys[7], BLOCKS).astype(jnp.int32),
    }


EPS = 1e-06

def spectral_weight(frequency, knee_part, slope_part, level_part):
    rising = jnp.power(frequency[None, :], slope_part[:, None])
    return rising / (rising + jnp.power(knee_part, slope_part)[:, None]) / (level_part * level_part)[:, None]

def reference(timelines, knee_freq, noise_slope, noise_level, templates, interval_bounds, block_index, block_slot):
    frequency = jnp.arange(SAMPLES // 2 + 1).astype(jnp.float32)
    det_group = DETS // 8

    def filter_rows(packed):
        det_rows, knee_part, slope_part, level_part = packed
        spectrum = jnp.fft.rfft(det_rows, axis=1)
        weight = spectral_weight(frequency, knee_part, slope_part, level_part)
        return jnp.fft.irfft(spectrum * weight, n=SAMPLES, axis=1).astype(jnp.float32)
    weighted = lax.map(filter_rows, (timelines.reshape(8, det_group, SAMPLES), knee_freq.reshape(8, det_group), noise_slope.reshape(8, det_group), noise_level.reshape(8, det_group)))
    weighted = weighted.reshape(DETS, SAMPLES)
    block_width = LONGEST
    block_count = SAMPLES // block_width
    highest = lax.Precision.HIGHEST

    def project(block_start):
        sample_block = lax.dynamic_slice_in_dim(weighted, block_start, block_width, 1)
        amplitudes = jnp.dot(templates.T, sample_block, precision=highest)
        return sample_block - jnp.dot(templates, amplitudes, precision=highest)
    pieces = lax.map(project, jnp.arange(block_count).astype(jnp.int32) * block_width)
    cleaned = jnp.transpose(pieces, (1, 0, 2)).reshape(DETS, SAMPLES)
    positions = jnp.arange(SAMPLES).astype(jnp.int32)
    sample_interval = lax.optimization_barrier(jnp.sum((positions[:, None] >= interval_bounds[None, 1:-1]).astype(jnp.int32), axis=1))
    indicator = (sample_interval[:, None] == jnp.arange(INTERVALS).astype(jnp.int32)[None, :]).astype(jnp.float32)
    power_sum = jnp.dot(cleaned * cleaned, indicator, precision=highest)
    interval_lens = (interval_bounds[1:] - interval_bounds[:-1]).astype(jnp.float32)
    variance = power_sum / interval_lens[None, :] + EPS
    segment_interval = sample_interval[::SEGLEN]
    per_segment = jnp.take(variance, segment_interval, axis=1)
    values = cleaned.reshape(DETS, SEGMENTS, SEGLEN) / per_segment[:, :, None]
    slot_ids = jnp.take(block_slot, block_index)
    owned_map = jax.ops.segment_sum(values.reshape(DETS * SEGMENTS, SEGLEN), slot_ids.reshape(DETS * SEGMENTS), num_segments=BLOCKS)
    return owned_map * (1.0 / math.sqrt(MEANHITS))
```

```python
import math

import jax
import jax.numpy as jnp
import numpy as np
from jax import lax
from jax.experimental import pallas as pl
from jax.experimental.pallas import tpu as pltpu
from jax.sharding import Mesh, PartitionSpec as P

DETS = 1024
SAMPLES = 32768
TEMPLATES = 512
SEGLEN = 128
SEGMENTS = 256
BLOCKS = 256
INTERVALS = 32
EPS = 1e-06
OWN_DETS = 4
HALF = SEGMENTS // 2
ROWS = HALF + 8
GROUP = 16
GROUPS = SEGMENTS // GROUP
MAP_SCALE = 1.0 / math.sqrt(DETS * SAMPLES // (SEGLEN * BLOCKS))
ALL = ("z", "yh", "yl", "x", "c")
bf16 = jnp.bfloat16
f32 = jnp.float32


def split_np(table):
    high = np.asarray(table, np.float32).astype(jnp.bfloat16)
    low = (table - high.astype(np.float64)).astype(np.float32).astype(jnp.bfloat16)
    return high, low


def tables():
    k = np.arange(HALF)
    c = np.arange(SEGMENTS)
    angle = 2.0 * np.pi * ((k[:, None] * c[None, :]) % SEGMENTS) / SEGMENTS
    outer = np.concatenate([np.cos(angle), -np.sin(angle)], axis=0)
    outer[HALF] = 1.0 - 2.0 * (c % 2)
    p = np.arange(SEGLEN)
    angle = 2.0 * np.pi * ((p[:, None] * p[None, :]) % SEGLEN) / SEGLEN
    inner = np.block([[np.cos(angle), -np.sin(angle)], [np.sin(angle), np.cos(angle)]])
    row = np.arange(ROWS)
    angle = 2.0 * np.pi * (row[:, None] * p[None, :]) / SAMPLES
    freq = row[:, None] + SEGMENTS * p[None, :]
    fold = np.minimum(freq, SAMPLES - freq)
    log_fold = np.where(fold > 0, np.log(np.maximum(fold, 1)), 0.0)
    return (
        *split_np(outer),
        *split_np(inner),
        np.cos(angle).astype(np.float32),
        np.sin(angle).astype(np.float32),
        log_fold.astype(np.float32),
    )


def split(value):
    high = value.astype(bf16)
    return high, (value - high.astype(f32)).astype(bf16)


def dot3(a, b, dims):
    def one(x, y):
        return lax.dot_general(x, y, (dims, ((), ())), preferred_element_type=f32)

    return one(a[0], b[0]) + (one(a[0], b[1]) + one(a[1], b[0]))


NN = ((1,), (0,))
NT = ((1,), (1,))
TN = ((0,), (0,))


def group_at(block):
    z, yh = divmod(block, 2)
    return 2 * z + (yh ^ (z & 1))


def weight_kernel(
    knee_ref, slope_ref, level_ref, x_ref, fh_ref, fl_ref, mh_ref, ml_ref, cos_ref, sin_ref, log_ref, out_ref
):
    parts = [split(x_ref[pl.ds(d, SEGMENTS, stride=OWN_DETS), :]) for d in range(OWN_DETS)]
    outer = (fh_ref[...], fl_ref[...])
    inner = (mh_ref[...], ml_ref[...])
    cos, sin, log_fold = cos_ref[...], sin_ref[...], log_ref[...]
    samples = tuple(jnp.concatenate([part[i] for part in parts], axis=1) for i in range(2))
    section = dot3(outer, samples, NN)
    top = lax.broadcasted_iota(jnp.int32, (8, SEGLEN), 0) == 0
    stacked = []
    for d in range(OWN_DETS):
        cut = slice(SEGLEN * d, SEGLEN * (d + 1))
        real, imag = section[:HALF, cut], section[HALF:, cut]
        real = jnp.concatenate([real, jnp.where(top, imag[:8], 0.0)], axis=0)
        imag = jnp.concatenate([jnp.where(top, 0.0, imag[:8]), imag[8:], jnp.zeros((8, SEGLEN), f32)], axis=0)
        stacked.append(jnp.concatenate([real * cos + imag * sin, imag * cos - real * sin], axis=1))
    spectrum = dot3(split(jnp.concatenate(stacked, axis=0)), inner, NN)
    row = lax.broadcasted_iota(jnp.int32, (ROWS, SEGLEN), 0)
    zero_freq = (row == 0) & (lax.broadcasted_iota(jnp.int32, (ROWS, SEGLEN), 1) == 0)
    times = jnp.where((row == 0) | (row == HALF), 1.0 / SAMPLES, 2.0 / SAMPLES).astype(f32)
    shaped = []
    for d in range(OWN_DETS):
        log_knee = jnp.log(jnp.full((1, SEGLEN), knee_ref[d], f32))
        slope = slope_ref[d]
        level = jnp.full((1, SEGLEN), level_ref[d], f32)
        ratio = jnp.exp(slope * (log_knee - log_fold))
        weight = jnp.where(zero_freq, 0.0, times / ((1.0 + ratio) * (level * level)))
        part = spectrum[ROWS * d : ROWS * (d + 1)]
        shaped.append(part * jnp.concatenate([weight, weight], axis=1))
    back = dot3(split(jnp.concatenate(shaped, axis=0)), inner, NT)
    turned = []
    for d in range(OWN_DETS):
        part = back[ROWS * d : ROWS * (d + 1)]
        real, imag = part[:, :SEGLEN], part[:, SEGLEN:]
        turn_re = real * cos - imag * sin
        turn_im = imag * cos + real * sin
        first = jnp.where(top, jnp.broadcast_to(turn_re[HALF : HALF + 1], (8, SEGLEN)), turn_im[:8])
        turned.append(jnp.concatenate([turn_re[:HALF], first, turn_im[8:HALF]], axis=0))
    result = dot3(outer, split(jnp.concatenate(turned, axis=1)), TN)
    for d in range(OWN_DETS):
        for block in range(GROUPS):
            start = GROUP * group_at(block)
            out_ref[pl.ds(GROUP * OWN_DETS * block + d, GROUP, stride=OWN_DETS), :] = result[
                start : start + GROUP, SEGLEN * d : SEGLEN * (d + 1)
            ]


def project_kernel(data_ref, templates_ref, clean_ref, power_ref):
    data = data_ref[...].T
    pattern = split(templates_ref[...])
    amplitudes = dot3(split(data), pattern, NN)
    cleaned = data - dot3(split(amplitudes), pattern, NT)
    clean_ref[...] = cleaned
    power = jnp.sum(cleaned * cleaned, axis=0, keepdims=True)
    power = jnp.concatenate([power[:, SEGLEN * k : SEGLEN * (k + 1)] for k in range(8)], axis=0)
    for member in range(GROUP):
        power_ref[member] = power


def interval_of(bounds_ref, segment):
    at = segment * SEGLEN
    first = jnp.int32(0)
    end = jnp.int32(SAMPLES)
    for t in range(1, INTERVALS):
        bound = bounds_ref[t]
        first = jnp.where(bound <= at, jnp.maximum(first, bound), first)
        end = jnp.where(bound > at, jnp.minimum(end, bound), end)
    return first // SEGLEN, end // SEGLEN


def masked_sum(gathered_ref, base, first, end):
    total = jnp.zeros((8, SEGLEN), f32)
    for member in range(GROUP):
        inside = (base + member >= first) & (base + member < end)
        total = total + jnp.where(inside, 1.0, 0.0) * gathered_ref[member]
    return total


def halo_kernel(bounds_ref, segment_ref, gathered_ref, own_ref, ahead_ref, behind_ref):
    segment = segment_ref[0]
    base = segment // GROUP * GROUP
    first, end = interval_of(bounds_ref, segment)
    own_ref[...] = masked_sum(gathered_ref, base, first, end)
    first, end = interval_of(bounds_ref, base + GROUP)
    ahead_ref[...] = masked_sum(gathered_ref, base, first, end)
    first, end = interval_of(bounds_ref, base - 1)
    behind_ref[...] = masked_sum(gathered_ref, base, jnp.where(base == 0, end, first), end)


def slot_kernel(segment_ref, index_ref, slot_ref, hot_ref):
    segment = segment_ref[0]
    pick = lax.broadcasted_iota(jnp.int32, (8, SEGMENTS), 1) == segment
    index = index_ref[...].astype(f32).astype(bf16)
    seen = lax.dot_general(
        jnp.where(pick, 1.0, 0.0).astype(bf16), index, (NT, ((), ())), preferred_element_type=f32
    )
    block = lax.broadcasted_iota(jnp.int32, (BLOCKS, DETS), 0)
    hot = jnp.where(jnp.broadcast_to(seen[0:1].astype(jnp.int32), (BLOCKS, DETS)) == block, 1.0, 0.0).astype(bf16)
    table = jnp.broadcast_to(slot_ref[...].astype(f32).astype(bf16), (8, BLOCKS))
    slot = lax.dot_general(table, hot, (NN, ((), ())), preferred_element_type=f32)
    row = ((block >> 3) & 7) * 32 + (block >> 6) * 8 + (block & 7)
    hot_ref[...] = jnp.where(
        jnp.broadcast_to(slot[0:1].astype(jnp.int32), (BLOCKS, DETS)) == row, 1.0, 0.0
    ).astype(bf16)


def bin_kernel(bounds_ref, segment_ref, clean_ref, own_ref, before_ref, after_ref, hot_ref, map_ref):
    segment = segment_ref[0]
    base = segment // GROUP * GROUP
    first, end = interval_of(bounds_ref, segment)
    total = own_ref[...]
    total = total + jnp.where(first < base, 1.0, 0.0) * before_ref[...]
    total = total + jnp.where(end > base + GROUP, 1.0, 0.0) * after_ref[...]
    length = jnp.full((8, SEGLEN), (end - first) * SEGLEN, jnp.int32).astype(f32)
    inverse = 1.0 / (total / length + EPS)
    values = jnp.concatenate(
        [clean_ref[:, SEGLEN * k : SEGLEN * (k + 1)] * inverse[k : k + 1] for k in range(8)], axis=1
    )
    high, low = split(values)
    hot = hot_ref[...]
    map_ref[...] = lax.dot_general(hot, high, (NT, ((), ())), preferred_element_type=f32) + lax.dot_general(
        hot, low, (NT, ((), ())), preferred_element_type=f32
    )


def fold_kernel(parts_ref, out_ref):
    total = parts_ref[0]
    for i in range(1, parts_ref.shape[0]):
        total = total + parts_ref[i]
    total = total * MAP_SCALE
    for i in range(out_ref.shape[0]):
        out_ref[i] = total


VMEM = pl.BlockSpec(memory_space=pltpu.VMEM)
SMEM = pl.BlockSpec(memory_space=pltpu.SMEM)


def call(kernel, specs, outs, name):
    shapes = [jax.ShapeDtypeStruct(shape, dtype) for shape, dtype in outs]
    return pl.pallas_call(
        kernel,
        out_shape=shapes if len(shapes) > 1 else shapes[0],
        in_specs=specs,
        out_specs=[VMEM] * len(shapes) if len(shapes) > 1 else VMEM,
        compiler_params=pltpu.CompilerParams(vmem_limit_bytes=32 * 1024 * 1024),
        name=name,
    )


def neighbour_pairs():
    at = {group_at(block): block for block in range(GROUPS)}
    ahead = []
    for g in range(GROUPS - 1):
        (z, yh), (z_to, yh_to) = divmod(at[g], 2), divmod(at[g + 1], 2)
        for yl in range(2):
            yl_to = yl if yh == yh_to else 1 - yl
            ahead.append(((z * 2 + yh) * 2 + yl, (z_to * 2 + yh_to) * 2 + yl_to))
    return ahead, [(b, a) for a, b in ahead]


def local(timelines, knee_freq, noise_slope, noise_level, templates, interval_bounds, block_index, block_slot):
    z, yh = lax.axis_index("z"), lax.axis_index("yh")
    member = lax.axis_index(("yl", "x", "c"))
    segment = ((2 * z + (yh ^ (z & 1))) * GROUP + member).astype(jnp.int32).reshape(1)
    rows = timelines.reshape(OWN_DETS, SEGMENTS, SEGLEN).transpose(1, 0, 2).reshape(DETS, SEGLEN)
    weighted = call(weight_kernel, [SMEM] * 3 + [VMEM] * 8, [((DETS, SEGLEN), f32)], "weight")(
        knee_freq, noise_slope, noise_level, rows, *[jnp.asarray(t) for t in tables()]
    )
    data = lax.all_to_all(
        weighted.reshape(SEGMENTS, OWN_DETS, SEGLEN), ALL, split_axis=0, concat_axis=0, tiled=True
    ).reshape(DETS, SEGLEN)
    cleaned, power = call(
        project_kernel, [VMEM] * 2, [((SEGLEN, DETS), f32), ((GROUP, 8, SEGLEN), f32)], "project"
    )(data, templates)
    gathered = lax.all_to_all(power, ("yl", "x", "c"), split_axis=0, concat_axis=0, tiled=True)
    own, ahead, behind = call(halo_kernel, [SMEM] * 2 + [VMEM], [((8, SEGLEN), f32)] * 3, "halo")(
        interval_bounds, segment, gathered
    )
    up, down = neighbour_pairs()
    before = lax.ppermute(ahead, ("z", "yh", "yl"), up)
    after = lax.ppermute(behind, ("z", "yh", "yl"), down)
    hot = call(slot_kernel, [SMEM] + [VMEM] * 2, [((BLOCKS, DETS), bf16)], "slots")(
        segment, block_index, block_slot.reshape(1, BLOCKS)
    )
    partial = call(bin_kernel, [SMEM] * 2 + [VMEM] * 5, [((BLOCKS, SEGLEN), f32)], "bin")(
        interval_bounds, segment, cleaned, own, before, after, hot
    )
    spread = lax.all_to_all(
        partial.reshape(32, 8, SEGLEN), ("yh", "yl", "x", "c"), split_axis=0, concat_axis=0, tiled=True
    )
    copies = call(fold_kernel, [VMEM], [((32, 8, SEGLEN), f32)], "fold")(spread)
    sums = lax.all_to_all(copies, ("z", "yh", "yl"), split_axis=0, concat_axis=0, tiled=True)
    return jnp.sum(sums.reshape(8, 32, SEGLEN), axis=0)


def solution(mesh):
    whole = Mesh(mesh.devices.reshape(8, 2, 2, 4, 2), ALL)
    return jax.shard_map(
        local,
        mesh=whole,
        in_specs=(P(ALL, None), P(ALL), P(ALL), P(ALL), P(), P(), P(), P()),
        out_specs=P(("x", "c"), None),
        check_vma=False,
    )
```

```python
import math

import jax
import jax.numpy as jnp
import numpy as np
from jax import lax
from jax.experimental import pallas as pl
from jax.experimental.pallas import tpu as pltpu
from jax.sharding import Mesh, PartitionSpec as P

DETS = 1024
SAMPLES = 32768
TEMPLATES = 512
SEGLEN = 128
SEGMENTS = 256
BLOCKS = 256
INTERVALS = 32
EPS = 1e-06
OWN_DETS = 4
HALF = SEGMENTS // 2
ROWS = HALF + 8
GROUP = 16
GROUPS = SEGMENTS // GROUP
PLANE = 2 * GROUP
MAP_SCALE = 1.0 / math.sqrt(DETS * SAMPLES // (SEGLEN * BLOCKS))
ALL = ("z", "yh", "yl", "x", "c")
bf16 = jnp.bfloat16
f32 = jnp.float32


def split_np(table):
    high = np.asarray(table, np.float32).astype(jnp.bfloat16)
    low = (table - high.astype(np.float64)).astype(np.float32).astype(jnp.bfloat16)
    return high, low


def tables():
    k = np.arange(HALF)
    c = np.arange(SEGMENTS)
    angle = 2.0 * np.pi * ((k[:, None] * c[None, :]) % SEGMENTS) / SEGMENTS
    outer = np.concatenate([np.cos(angle), -np.sin(angle)], axis=0)
    outer[HALF] = 1.0 - 2.0 * (c % 2)
    p = np.arange(SEGLEN)
    angle = 2.0 * np.pi * ((p[:, None] * p[None, :]) % SEGLEN) / SEGLEN
    inner = np.block([[np.cos(angle), -np.sin(angle)], [np.sin(angle), np.cos(angle)]])
    row = np.arange(ROWS)
    angle = 2.0 * np.pi * (row[:, None] * p[None, :]) / SAMPLES
    freq = row[:, None] + SEGMENTS * p[None, :]
    fold = np.minimum(freq, SAMPLES - freq)
    log_fold = np.where(fold > 0, np.log(np.maximum(fold, 1)), 0.0)
    return (
        np.stack([*split_np(outer), *split_np(inner)]),
        np.stack([np.cos(angle), np.sin(angle), log_fold]).astype(np.float32),
    )


def split(value):
    high = value.astype(bf16)
    return high, (value - high.astype(f32)).astype(bf16)


def dot3(a, b, dims):
    def one(x, y):
        return lax.dot_general(x, y, (dims, ((), ())), preferred_element_type=f32)

    return one(a[0], b[0]) + (one(a[0], b[1]) + one(a[1], b[0]))


NN = ((1,), (0,))
NT = ((1,), (1,))
TN = ((0,), (0,))


def group_at(block):
    z, yh = divmod(block, 2)
    return 2 * z + (yh ^ (z & 1))


def weight_kernel(
    knee_hbm, slope_hbm, level_hbm, x_hbm, tables_hbm, factors_hbm, out_ref,
    knee_ref, slope_ref, level_ref, x_ref, tables_ref, factors_ref, sems,
):
    pairs = [
        (x_hbm, x_ref),
        (tables_hbm, tables_ref),
        (factors_hbm, factors_ref),
        (knee_hbm, knee_ref),
        (slope_hbm, slope_ref),
        (level_hbm, level_ref),
    ]
    copies = [pltpu.make_async_copy(src, dst, sems.at[i]) for i, (src, dst) in enumerate(pairs)]
    for copy in copies:
        copy.start()
    for copy in copies:
        copy.wait()
    parts = [split(x_ref[pl.ds(d, SEGMENTS, stride=OWN_DETS), :]) for d in range(OWN_DETS)]
    outer = (tables_ref[0], tables_ref[1])
    inner = (tables_ref[2], tables_ref[3])
    cos, sin, log_fold = factors_ref[0], factors_ref[1], factors_ref[2]
    samples = tuple(jnp.concatenate([part[i] for part in parts], axis=1) for i in range(2))
    section = dot3(outer, samples, NN)
    top = lax.broadcasted_iota(jnp.int32, (8, SEGLEN), 0) == 0
    stacked = []
    for d in range(OWN_DETS):
        cut = slice(SEGLEN * d, SEGLEN * (d + 1))
        real, imag = section[:HALF, cut], section[HALF:, cut]
        real = jnp.concatenate([real, jnp.where(top, imag[:8], 0.0)], axis=0)
        imag = jnp.concatenate([jnp.where(top, 0.0, imag[:8]), imag[8:], jnp.zeros((8, SEGLEN), f32)], axis=0)
        stacked.append(jnp.concatenate([real * cos + imag * sin, imag * cos - real * sin], axis=1))
    spectrum = dot3(split(jnp.concatenate(stacked, axis=0)), inner, NN)
    row = lax.broadcasted_iota(jnp.int32, (ROWS, SEGLEN), 0)
    zero_freq = (row == 0) & (lax.broadcasted_iota(jnp.int32, (ROWS, SEGLEN), 1) == 0)
    times = jnp.where((row == 0) | (row == HALF), 1.0 / SAMPLES, 2.0 / SAMPLES).astype(f32)
    shaped = []
    for d in range(OWN_DETS):
        log_knee = jnp.log(jnp.full((1, SEGLEN), knee_ref[d], f32))
        slope = slope_ref[d]
        level = jnp.full((1, SEGLEN), level_ref[d], f32)
        ratio = jnp.exp(slope * (log_knee - log_fold))
        weight = jnp.where(zero_freq, 0.0, times / ((1.0 + ratio) * (level * level)))
        part = spectrum[ROWS * d : ROWS * (d + 1)]
        shaped.append(part * jnp.concatenate([weight, weight], axis=1))
    back = dot3(split(jnp.concatenate(shaped, axis=0)), inner, NT)
    turned = []
    for d in range(OWN_DETS):
        part = back[ROWS * d : ROWS * (d + 1)]
        real, imag = part[:, :SEGLEN], part[:, SEGLEN:]
        turn_re = real * cos - imag * sin
        turn_im = imag * cos + real * sin
        first = jnp.where(top, jnp.broadcast_to(turn_re[HALF : HALF + 1], (8, SEGLEN)), turn_im[:8])
        turned.append(jnp.concatenate([turn_re[:HALF], first, turn_im[8:HALF]], axis=0))
    result = dot3(outer, split(jnp.concatenate(turned, axis=1)), TN)
    for d in range(OWN_DETS):
        for block in range(GROUPS):
            start = GROUP * group_at(block)
            out_ref[pl.ds(GROUP * OWN_DETS * block + d, GROUP, stride=OWN_DETS), :] = result[
                start : start + GROUP, SEGLEN * d : SEGLEN * (d + 1)
            ]


def slot_kernel(segment_ref, index_ref, slot_ref, hot_ref):
    pick = lax.broadcasted_iota(jnp.int32, (8, SEGMENTS), 1) == segment_ref[0]
    index = index_ref[...].astype(f32).astype(bf16)
    seen = lax.dot_general(
        jnp.where(pick, 1.0, 0.0).astype(bf16), index, (NT, ((), ())), preferred_element_type=f32
    )
    block = lax.broadcasted_iota(jnp.int32, (BLOCKS, DETS), 0)
    hot = jnp.where(jnp.broadcast_to(seen[0:1].astype(jnp.int32), (BLOCKS, DETS)) == block, 1.0, 0.0).astype(bf16)
    table = jnp.broadcast_to(slot_ref[...].astype(f32).astype(bf16), (8, BLOCKS))
    slot = lax.dot_general(table, hot, (NN, ((), ())), preferred_element_type=f32)
    row = ((block >> 3) & 7) * 32 + (block >> 6) * 8 + (block & 7)
    hot_ref[...] = jnp.where(
        jnp.broadcast_to(slot[0:1].astype(jnp.int32), (BLOCKS, DETS)) == row, 1.0, 0.0
    ).astype(bf16)


def project_kernel(data_ref, templates_ref, clean_ref, power_ref):
    data = data_ref[...].T
    pattern = split(templates_ref[...])
    amplitudes = dot3(split(data), pattern, NN)
    cleaned = data - dot3(split(amplitudes), pattern, NT)
    clean_ref[...] = cleaned
    power = jnp.sum(cleaned * cleaned, axis=0, keepdims=True)
    power = jnp.concatenate([power[:, SEGLEN * k : SEGLEN * (k + 1)] for k in range(8)], axis=0)
    for member in range(PLANE):
        power_ref[member] = power


def interval_of(bounds_ref, segment):
    at = segment * SEGLEN
    first = jnp.int32(0)
    end = jnp.int32(SAMPLES)
    for t in range(1, INTERVALS):
        bound = bounds_ref[t]
        first = jnp.where(bound <= at, jnp.maximum(first, bound), first)
        end = jnp.where(bound > at, jnp.minimum(end, bound), end)
    return first // SEGLEN, end // SEGLEN


def masked_sum(gathered_ref, base, turn, first, end):
    total = jnp.zeros((8, SEGLEN), f32)
    for member in range(PLANE):
        at = base + (member ^ turn)
        inside = (at >= first) & (at < end)
        total = total + jnp.where(inside, 1.0, 0.0) * gathered_ref[member]
    return total


def halo_kernel(bounds_ref, segment_ref, gathered_ref, own_ref, share_ref, message_ref):
    segment = segment_ref[0]
    plane = segment // PLANE
    base = plane * PLANE
    turn = (plane & 1) * GROUP
    late = (segment & GROUP) != 0
    first, end = interval_of(bounds_ref, segment)
    length = jnp.full((8, SEGLEN), (end - first) * SEGLEN, jnp.int32).astype(f32)
    own_ref[...] = masked_sum(gathered_ref, base, turn, first, end) / length + EPS
    beyond = jnp.where(late, end > base + PLANE, first < base)
    share_ref[...] = jnp.where(beyond, 1.0, 0.0) / length
    first, end = interval_of(bounds_ref, jnp.where(late, base + PLANE, base - 1))
    edge = jnp.where(late, base + PLANE == SEGMENTS, base == 0)
    message_ref[...] = masked_sum(gathered_ref, base, turn, jnp.where(edge, end, first), end)


def bin_kernel(clean_ref, own_ref, share_ref, message_ref, hot_ref, map_ref):
    inverse = 1.0 / (own_ref[...] + share_ref[...] * message_ref[...])
    values = jnp.concatenate(
        [clean_ref[:, SEGLEN * k : SEGLEN * (k + 1)] * inverse[k : k + 1] for k in range(8)], axis=1
    )
    high, low = split(values)
    hot = hot_ref[...]
    map_ref[...] = lax.dot_general(hot, high, (NT, ((), ())), preferred_element_type=f32) + lax.dot_general(
        hot, low, (NT, ((), ())), preferred_element_type=f32
    )


def fold_kernel(parts_ref, out_ref):
    total = parts_ref[0]
    for i in range(1, parts_ref.shape[0]):
        total = total + parts_ref[i]
    total = total * MAP_SCALE
    for i in range(out_ref.shape[0]):
        out_ref[i] = total


VMEM = pl.BlockSpec(memory_space=pltpu.VMEM)
SMEM = pl.BlockSpec(memory_space=pltpu.SMEM)
HBM = pl.BlockSpec(memory_space=pltpu.HBM)


def call(kernel, specs, outs, name, scratch=(), mib=16):
    shapes = [jax.ShapeDtypeStruct(shape, dtype) for shape, dtype in outs]
    return pl.pallas_call(
        kernel,
        out_shape=shapes if len(shapes) > 1 else shapes[0],
        in_specs=specs,
        out_specs=[VMEM] * len(shapes) if len(shapes) > 1 else VMEM,
        scratch_shapes=list(scratch),
        compiler_params=pltpu.CompilerParams(vmem_limit_bytes=mib * 1024 * 1024),
        name=name,
    )


def swap_pairs():
    pairs = []
    for z in range(8):
        for yh in range(2):
            z_to = z ^ 1 if yh else (z + (1 if z % 2 else -1)) % 8
            pairs.append((2 * z + yh, 2 * z_to + yh))
    return pairs


def local(timelines, knee_freq, noise_slope, noise_level, templates, interval_bounds, block_index, block_slot):
    z, yh = lax.axis_index("z"), lax.axis_index("yh")
    member = lax.axis_index(("yl", "x", "c"))
    segment = ((2 * z + (yh ^ (z & 1))) * GROUP + member).astype(jnp.int32).reshape(1)
    rows = timelines.reshape(OWN_DETS, SEGMENTS, SEGLEN).transpose(1, 0, 2).reshape(DETS, SEGLEN)
    scratch = [pltpu.SMEM((OWN_DETS,), f32)] * 3 + [
        pltpu.VMEM((DETS, SEGLEN), f32),
        pltpu.VMEM((4, SEGMENTS, SEGMENTS), bf16),
        pltpu.VMEM((3, ROWS, SEGLEN), f32),
        pltpu.SemaphoreType.DMA((6,)),
    ]
    weighted = call(weight_kernel, [HBM] * 6, [((DETS, SEGLEN), f32)], "weight", scratch, 60)(
        knee_freq, noise_slope, noise_level, rows, *[jnp.asarray(t) for t in tables()]
    )
    data = lax.all_to_all(
        weighted.reshape(SEGMENTS, OWN_DETS, SEGLEN), ALL, split_axis=0, concat_axis=0, tiled=True
    ).reshape(DETS, SEGLEN)
    hot = call(slot_kernel, [SMEM] + [VMEM] * 2, [((BLOCKS, DETS), bf16)], "slots")(
        segment, block_index, block_slot.reshape(1, BLOCKS)
    )
    cleaned, power = call(
        project_kernel, [VMEM] * 2, [((SEGLEN, DETS), f32), ((PLANE, 8, SEGLEN), f32)], "project"
    )(data, templates)
    gathered = lax.all_to_all(power, ("yh", "yl", "x", "c"), split_axis=0, concat_axis=0, tiled=True)
    own, share, message = call(halo_kernel, [SMEM] * 2 + [VMEM], [((8, SEGLEN), f32)] * 3, "halo")(
        interval_bounds, segment, gathered
    )
    beyond = lax.ppermute(message, ("z", "yh"), swap_pairs())
    partial = call(bin_kernel, [VMEM] * 5, [((BLOCKS, SEGLEN), f32)], "bin")(cleaned, own, share, beyond, hot)
    spread = lax.all_to_all(
        partial.reshape(32, 8, SEGLEN), ("yh", "yl", "x", "c"), split_axis=0, concat_axis=0, tiled=True
    )
    copies = call(fold_kernel, [VMEM], [((32, 8, SEGLEN), f32)], "fold")(spread)
    sums = lax.all_to_all(copies, ("z", "yh", "yl"), split_axis=0, concat_axis=0, tiled=True)
    return jnp.sum(sums.reshape(8, 32, SEGLEN), axis=0)


def solution(mesh):
    whole = Mesh(mesh.devices.reshape(8, 2, 2, 4, 2), ALL)
    return jax.shard_map(
        local,
        mesh=whole,
        in_specs=(P(ALL, None), P(ALL), P(ALL), P(ALL), P(), P(), P(), P()),
        out_specs=P(("x", "c"), None),
        check_vma=False,
    )
```

```python
import math

import jax
import jax.numpy as jnp
import numpy as np
from jax import lax
from jax.experimental import pallas as pl
from jax.experimental.pallas import tpu as pltpu
from jax.sharding import Mesh, PartitionSpec as P

DETS = 1024
SAMPLES = 32768
TEMPLATES = 512
SEGLEN = 128
SEGMENTS = 256
BLOCKS = 256
INTERVALS = 32
EPS = 1e-06
OWN_DETS = 4
HALF = SEGMENTS // 2
ROWS = HALF + 8
GROUP = 16
PLANE = 2 * GROUP
MAP_SCALE = 1.0 / math.sqrt(DETS * SAMPLES // (SEGLEN * BLOCKS))
ALL = ("z", "y", "x", "c")
PLANES = 8
bf16 = jnp.bfloat16
f32 = jnp.float32


def split_np(table):
    high = np.asarray(table, np.float32).astype(jnp.bfloat16)
    low = (table - high.astype(np.float64)).astype(np.float32).astype(jnp.bfloat16)
    return high, low


def tables():
    k = np.arange(HALF)
    c = np.arange(SEGMENTS)
    angle = 2.0 * np.pi * ((k[:, None] * c[None, :]) % SEGMENTS) / SEGMENTS
    outer = np.concatenate([np.cos(angle), -np.sin(angle)], axis=0)
    outer[HALF] = 1.0 - 2.0 * (c % 2)
    p = np.arange(SEGLEN)
    angle = 2.0 * np.pi * ((p[:, None] * p[None, :]) % SEGLEN) / SEGLEN
    inner = np.block([[np.cos(angle), -np.sin(angle)], [np.sin(angle), np.cos(angle)]])
    row = np.arange(ROWS)
    angle = 2.0 * np.pi * (row[:, None] * p[None, :]) / SAMPLES
    freq = row[:, None] + SEGMENTS * p[None, :]
    fold = np.minimum(freq, SAMPLES - freq)
    log_fold = np.where(fold > 0, np.log(np.maximum(fold, 1)), 0.0)
    return (
        np.stack([*split_np(outer), *split_np(inner)]),
        np.stack([np.cos(angle), np.sin(angle), log_fold]).astype(np.float32),
    )


def split(value):
    high = value.astype(bf16)
    return high, (value - high.astype(f32)).astype(bf16)


def dot3(a, b, dims):
    def one(x, y):
        return lax.dot_general(x, y, (dims, ((), ())), preferred_element_type=f32)

    return one(a[0], b[0]) + (one(a[0], b[1]) + one(a[1], b[0]))


NN = ((1,), (0,))
NT = ((1,), (1,))
TN = ((0,), (0,))


def held_at(plane, core):
    return PLANE * ((plane + core) % PLANES) + GROUP * (1 - core)


def weight_kernel(
    knee_hbm, slope_hbm, level_hbm, x_hbm, tables_hbm, factors_hbm, out_hbm,
    knee_ref, slope_ref, level_ref, x_ref, outer_ref, inner_ref, factors_ref, out_ref, sems, out_sems,
):
    pairs = [
        (x_hbm, x_ref),
        (tables_hbm.at[pl.ds(0, 2)], outer_ref),
        (factors_hbm, factors_ref),
        (tables_hbm.at[pl.ds(2, 2)], inner_ref),
        (knee_hbm, knee_ref),
        (slope_hbm, slope_ref),
        (level_hbm, level_ref),
    ]
    copies = [pltpu.make_async_copy(src, dst, sems.at[i]) for i, (src, dst) in enumerate(pairs)]
    for copy in copies:
        copy.start()
    copies[0].wait()
    copies[1].wait()
    parts = [split(x_ref[pl.ds(d, SEGMENTS, stride=OWN_DETS), :]) for d in range(OWN_DETS)]
    outer = (outer_ref[0], outer_ref[1])
    samples = tuple(jnp.concatenate([part[i] for part in parts], axis=1) for i in range(2))
    section = dot3(outer, samples, NN)
    for copy in copies[2:]:
        copy.wait()
    inner = (inner_ref[0], inner_ref[1])
    cos, sin, log_fold = factors_ref[0], factors_ref[1], factors_ref[2]
    top = lax.broadcasted_iota(jnp.int32, (8, SEGLEN), 0) == 0
    stacked = []
    for d in range(OWN_DETS):
        cut = slice(SEGLEN * d, SEGLEN * (d + 1))
        real, imag = section[:HALF, cut], section[HALF:, cut]
        real = jnp.concatenate([real, jnp.where(top, imag[:8], 0.0)], axis=0)
        imag = jnp.concatenate([jnp.where(top, 0.0, imag[:8]), imag[8:], jnp.zeros((8, SEGLEN), f32)], axis=0)
        stacked.append(jnp.concatenate([real * cos + imag * sin, imag * cos - real * sin], axis=1))
    spectrum = dot3(split(jnp.concatenate(stacked, axis=0)), inner, NN)
    row = lax.broadcasted_iota(jnp.int32, (ROWS, SEGLEN), 0)
    zero_freq = (row == 0) & (lax.broadcasted_iota(jnp.int32, (ROWS, SEGLEN), 1) == 0)
    times = jnp.where((row == 0) | (row == HALF), 1.0 / SAMPLES, 2.0 / SAMPLES).astype(f32)
    shaped = []
    for d in range(OWN_DETS):
        log_knee = jnp.log(jnp.full((1, SEGLEN), knee_ref[d], f32))
        slope = slope_ref[d]
        level = jnp.full((1, SEGLEN), level_ref[d], f32)
        ratio = jnp.exp(slope * (log_knee - log_fold))
        weight = jnp.where(zero_freq, 0.0, times / ((1.0 + ratio) * (level * level)))
        part = spectrum[ROWS * d : ROWS * (d + 1)]
        shaped.append(part * jnp.concatenate([weight, weight], axis=1))
    back = dot3(split(jnp.concatenate(shaped, axis=0)), inner, NT)
    turned = []
    for d in range(OWN_DETS):
        part = back[ROWS * d : ROWS * (d + 1)]
        real, imag = part[:, :SEGLEN], part[:, SEGLEN:]
        turn_re = real * cos - imag * sin
        turn_im = imag * cos + real * sin
        first = jnp.where(top, jnp.broadcast_to(turn_re[HALF : HALF + 1], (8, SEGLEN)), turn_im[:8])
        turned.append(jnp.concatenate([turn_re[:HALF], first, turn_im[8:HALF]], axis=0))
    result = dot3(outer, split(jnp.concatenate(turned, axis=1)), TN)
    writes = []
    for plane in range(PLANES):
        for core in range(2):
            start = held_at(plane, core)
            for d in range(OWN_DETS):
                row = (PLANE * plane + core) * OWN_DETS + d
                out_ref[pl.ds(row, GROUP, stride=2 * OWN_DETS), :] = result[
                    start : start + GROUP, SEGLEN * d : SEGLEN * (d + 1)
                ]
        rows = pl.ds(PLANE * OWN_DETS * plane, PLANE * OWN_DETS)
        writes.append(pltpu.make_async_copy(out_ref.at[rows], out_hbm.at[rows], out_sems.at[plane]))
        writes[-1].start()
    for write in writes:
        write.wait()


def project_kernel(data_ref, templates_ref, clean_ref, power_ref):
    data = data_ref[...].T
    pattern = split(templates_ref[...])
    amplitudes = dot3(split(data), pattern, NN)
    cleaned = data - dot3(split(amplitudes), pattern, NT)
    clean_ref[...] = cleaned
    power = jnp.sum(cleaned * cleaned, axis=0, keepdims=True)
    power = jnp.concatenate([power[:, SEGLEN * k : SEGLEN * (k + 1)] for k in range(8)], axis=0)
    for member in range(PLANE):
        power_ref[member] = power


def interval_of(bounds_ref, segment):
    at = segment * SEGLEN
    first = jnp.int32(0)
    end = jnp.int32(SAMPLES)
    for t in range(1, INTERVALS):
        bound = bounds_ref[t]
        first = jnp.where(bound <= at, jnp.maximum(first, bound), first)
        end = jnp.where(bound > at, jnp.minimum(end, bound), end)
    return first // SEGLEN, end // SEGLEN


def prepare_kernel(
    segment_ref, bounds_ref, index_ref, slot_ref, hot_ref, weight_ref, beyond_ref, share_ref
):
    segment = segment_ref[0]
    base = segment // PLANE * PLANE
    late = (segment & GROUP) != 0
    first, end = interval_of(bounds_ref, segment)
    part = 1.0 / jnp.full((8, SEGLEN), (end - first) * SEGLEN, jnp.int32).astype(f32)
    share_ref[...] = jnp.where(jnp.where(late, end > base + PLANE, first < base), part, 0.0)
    next_first, next_end = interval_of(bounds_ref, jnp.where(late, base + PLANE, base - 1))
    edge = jnp.where(late, base + PLANE == SEGMENTS, base == 0)
    next_first = jnp.where(edge, next_end, next_first)
    for member in range(PLANE):
        at = base + member
        weight_ref[member] = jnp.where((at >= first) & (at < end), part, 0.0)
        beyond_ref[member] = jnp.full((8, SEGLEN), jnp.where((at >= next_first) & (at < next_end), 1.0, 0.0), f32)
    pick = lax.broadcasted_iota(jnp.int32, (8, SEGMENTS), 1) == segment
    index = index_ref[...].astype(f32).astype(bf16)
    seen = lax.dot_general(
        jnp.where(pick, 1.0, 0.0).astype(bf16), index, (NT, ((), ())), preferred_element_type=f32
    )
    block = lax.broadcasted_iota(jnp.int32, (BLOCKS, DETS), 0)
    hot = jnp.where(jnp.broadcast_to(seen[0:1].astype(jnp.int32), (BLOCKS, DETS)) == block, 1.0, 0.0).astype(bf16)
    table = jnp.broadcast_to(slot_ref[...].astype(f32).astype(bf16), (8, BLOCKS))
    slot = lax.dot_general(table, hot, (NN, ((), ())), preferred_element_type=f32)
    row = ((block >> 3) & 7) * 32 + (block >> 6) * 8 + (block & 7)
    hot_ref[...] = jnp.where(
        jnp.broadcast_to(slot[0:1].astype(jnp.int32), (BLOCKS, DETS)) == row, 1.0, 0.0
    ).astype(bf16)


def halo_kernel(gathered_ref, weight_ref, beyond_ref, own_ref, message_ref):
    own = jnp.full((8, SEGLEN), EPS, f32)
    message = jnp.zeros((8, SEGLEN), f32)
    for member in range(PLANE):
        power = gathered_ref[member]
        own = own + weight_ref[member] * power
        message = message + beyond_ref[member] * power
    own_ref[...] = own
    message_ref[...] = message


def bin_kernel(clean_ref, own_ref, share_ref, message_ref, hot_ref, map_ref):
    inverse = 1.0 / (own_ref[...] + share_ref[...] * message_ref[...])
    values = jnp.concatenate(
        [clean_ref[:, SEGLEN * k : SEGLEN * (k + 1)] * inverse[k : k + 1] for k in range(8)], axis=1
    )
    high, low = split(values)
    hot = hot_ref[...]
    map_ref[...] = lax.dot_general(hot, high, (NT, ((), ())), preferred_element_type=f32) + lax.dot_general(
        hot, low, (NT, ((), ())), preferred_element_type=f32
    )


def fold_kernel(parts_ref, out_ref):
    total = parts_ref[0]
    for i in range(1, parts_ref.shape[0]):
        total = total + parts_ref[i]
    total = total * MAP_SCALE
    for i in range(out_ref.shape[0]):
        out_ref[i] = total


VMEM = pl.BlockSpec(memory_space=pltpu.VMEM)
SMEM = pl.BlockSpec(memory_space=pltpu.SMEM)
HBM = pl.BlockSpec(memory_space=pltpu.HBM)


def call(kernel, specs, outs, name, scratch=(), mib=16, out_spec=VMEM):
    shapes = [jax.ShapeDtypeStruct(shape, dtype) for shape, dtype in outs]
    return pl.pallas_call(
        kernel,
        out_shape=shapes if len(shapes) > 1 else shapes[0],
        in_specs=specs,
        out_specs=[out_spec] * len(shapes) if len(shapes) > 1 else out_spec,
        scratch_shapes=list(scratch),
        compiler_params=pltpu.CompilerParams(vmem_limit_bytes=mib * 1024 * 1024),
        name=name,
    )


def interval_groups():
    groups = []
    for k in range(PLANES):
        early = [PLANE * ((k - 1) % PLANES) + 2 * m + 1 for m in range(GROUP)]
        groups.append(early + [PLANE * k + 2 * m for m in range(GROUP)])
    return groups


def local(timelines, knee_freq, noise_slope, noise_level, templates, interval_bounds, block_index, block_slot):
    core = lax.axis_index("c")
    group = lax.rem(lax.axis_index("z") + core, PLANES)
    segment = (PLANE * group + GROUP * (1 - core) + lax.axis_index(("y", "x"))).astype(jnp.int32).reshape(1)
    rows = timelines.reshape(OWN_DETS, SEGMENTS, SEGLEN).transpose(1, 0, 2).reshape(DETS, SEGLEN)
    scratch = [pltpu.SMEM((OWN_DETS,), f32)] * 3 + [
        pltpu.VMEM((DETS, SEGLEN), f32),
        pltpu.VMEM((2, SEGMENTS, SEGMENTS), bf16),
        pltpu.VMEM((2, SEGMENTS, SEGMENTS), bf16),
        pltpu.VMEM((3, ROWS, SEGLEN), f32),
        pltpu.VMEM((DETS, SEGLEN), f32),
        pltpu.SemaphoreType.DMA((7,)),
        pltpu.SemaphoreType.DMA((PLANES,)),
    ]
    weighted = call(weight_kernel, [HBM] * 6, [((DETS, SEGLEN), f32)], "weight", scratch, 60, HBM)(
        knee_freq, noise_slope, noise_level, rows, *[jnp.asarray(t) for t in tables()]
    )
    data = lax.all_to_all(
        weighted.reshape(SEGMENTS, OWN_DETS, SEGLEN), ALL, split_axis=0, concat_axis=0, tiled=True
    ).reshape(DETS, SEGLEN)
    line, lines = ((8, SEGLEN), f32), ((PLANE, 8, SEGLEN), f32)
    cleaned, power = call(project_kernel, [VMEM] * 2, [((SEGLEN, DETS), f32), lines], "project")(data, templates)
    gathered = lax.all_to_all(
        power, ALL, split_axis=0, concat_axis=0, axis_index_groups=interval_groups(), tiled=True
    )
    hot, inside, outside, share = call(
        prepare_kernel, [SMEM] * 2 + [VMEM] * 2, [((BLOCKS, DETS), bf16), lines, lines, line], "prepare"
    )(segment, interval_bounds, block_index, block_slot.reshape(1, BLOCKS))
    own, message = call(halo_kernel, [VMEM] * 3, [line] * 2, "halo")(gathered, inside, outside)
    beyond = lax.ppermute(message, "c", [(0, 1), (1, 0)])
    partial = call(bin_kernel, [VMEM] * 5, [((BLOCKS, SEGLEN), f32)], "bin")(cleaned, own, share, beyond, hot)
    spread = lax.all_to_all(
        partial.reshape(32, 8, SEGLEN), ("y", "x", "c"), split_axis=0, concat_axis=0, tiled=True
    )
    copies = call(fold_kernel, [VMEM], [((32, 8, SEGLEN), f32)], "fold")(spread)
    sums = lax.all_to_all(copies, ("z", "y"), split_axis=0, concat_axis=0, tiled=True)
    return jnp.sum(sums.reshape(8, 32, SEGLEN), axis=0)


def solution(mesh):
    whole = Mesh(mesh.devices.reshape(8, 4, 4, 2), ALL)
    return jax.shard_map(
        local,
        mesh=whole,
        in_specs=(P(ALL, None), P(ALL), P(ALL), P(ALL), P(), P(), P(), P()),
        out_specs=P(("x", "c"), None),
        check_vma=False,
    )
```

```python
import math

import jax
import jax.numpy as jnp
import numpy as np
from jax import lax
from jax.experimental import pallas as pl
from jax.experimental.pallas import tpu as pltpu
from jax.sharding import Mesh, PartitionSpec as P

DETS = 1024
SAMPLES = 32768
TEMPLATES = 512
SEGLEN = 128
SEGMENTS = 256
BLOCKS = 256
INTERVALS = 32
EPS = 1e-06
OWN_DETS = 4
HALF = SEGMENTS // 2
ROWS = HALF + 8
GROUP = 16
PLANE = 2 * GROUP
MAP_SCALE = 1.0 / math.sqrt(DETS * SAMPLES // (SEGLEN * BLOCKS))
ALL = ("z", "y", "x", "c")
PLANES = 8
bf16 = jnp.bfloat16
f32 = jnp.float32


def split_np(table):
    high = np.asarray(table, np.float32).astype(jnp.bfloat16)
    low = (table - high.astype(np.float64)).astype(np.float32).astype(jnp.bfloat16)
    return high, low


def tables():
    k = np.arange(HALF)
    c = np.arange(SEGMENTS)
    angle = 2.0 * np.pi * ((k[:, None] * c[None, :]) % SEGMENTS) / SEGMENTS
    outer = np.concatenate([np.cos(angle), -np.sin(angle)], axis=0)
    outer[HALF] = 1.0 - 2.0 * (c % 2)
    p = np.arange(SEGLEN)
    angle = 2.0 * np.pi * ((p[:, None] * p[None, :]) % SEGLEN) / SEGLEN
    inner = np.block([[np.cos(angle), -np.sin(angle)], [np.sin(angle), np.cos(angle)]])
    row = np.arange(ROWS)
    angle = 2.0 * np.pi * (row[:, None] * p[None, :]) / SAMPLES
    freq = row[:, None] + SEGMENTS * p[None, :]
    fold = np.minimum(freq, SAMPLES - freq)
    log_fold = np.where(fold > 0, np.log(np.maximum(fold, 1)), 0.0)
    return (
        np.stack([*split_np(outer), *split_np(inner), *split_np(outer.T)]),
        np.stack([np.cos(angle), np.sin(angle), log_fold]).astype(np.float32),
    )


def split(value):
    high = value.astype(bf16)
    return high, (value - high.astype(f32)).astype(bf16)


def dot3(a, b, dims):
    def one(x, y):
        return lax.dot_general(x, y, (dims, ((), ())), preferred_element_type=f32)

    rows = a[0].shape[0]
    both = one(jnp.concatenate(a, axis=0), b[0])
    return both[:rows] + (both[rows:] + one(a[0], b[1]))


NN = ((1,), (0,))
NT = ((1,), (1,))


def held_at(plane, core):
    return PLANE * ((plane + core) % PLANES) + GROUP * (1 - core)


def interval_of(bounds_ref, segment):
    at = segment * SEGLEN
    first = jnp.int32(0)
    end = jnp.int32(SAMPLES)
    for t in range(1, INTERVALS):
        bound = bounds_ref[t]
        first = jnp.where(bound <= at, jnp.maximum(first, bound), first)
        end = jnp.where(bound > at, jnp.minimum(end, bound), end)
    return first // SEGLEN, end // SEGLEN


def member_weights(bounds_ref, inside_ref, outside_ref, share_ref):
    core = lax.axis_index("c")
    base = PLANE * lax.rem(lax.axis_index("z") + core, PLANES)
    segment = base + GROUP * (1 - core) + 4 * lax.axis_index("y") + lax.axis_index("x")
    late = core == 0
    first, end = interval_of(bounds_ref, segment)
    part = 1.0 / jnp.full((8, SEGLEN), (end - first) * SEGLEN, jnp.int32).astype(f32)
    share_ref[...] = jnp.where(jnp.where(late, end > base + PLANE, first < base), part, 0.0)
    next_first, next_end = interval_of(bounds_ref, jnp.where(late, base + PLANE, base - 1))
    edge = jnp.where(late, base + PLANE == SEGMENTS, base == 0)
    next_first = jnp.where(edge, next_end, next_first)
    for member in range(PLANE):
        at = base + member
        inside_ref[member] = jnp.where((at >= first) & (at < end), part, 0.0)
        outside_ref[member] = jnp.full((8, SEGLEN), jnp.where((at >= next_first) & (at < next_end), 1.0, 0.0), f32)


def weight_kernel(
    bounds_hbm, knee_hbm, slope_hbm, level_hbm, x_hbm, tables_hbm, factors_hbm,
    out_ref, inside_ref, outside_ref, share_ref,
    bounds_ref, knee_ref, slope_ref, level_ref, x_ref, outer_ref, inner_ref, back_ref, factors_ref, sems,
):
    pairs = [
        (bounds_hbm, bounds_ref),
        (x_hbm, x_ref),
        (tables_hbm.at[pl.ds(0, 2)], outer_ref),
        (factors_hbm, factors_ref),
        (tables_hbm.at[pl.ds(2, 2)], inner_ref),
        (knee_hbm, knee_ref),
        (slope_hbm, slope_ref),
        (level_hbm, level_ref),
        (tables_hbm.at[pl.ds(4, 2)], back_ref),
    ]
    copies = [pltpu.make_async_copy(src, dst, sems.at[i]) for i, (src, dst) in enumerate(pairs)]
    for copy in copies:
        copy.start()
    copies[0].wait()
    member_weights(bounds_ref, inside_ref, outside_ref, share_ref)
    copies[1].wait()
    copies[2].wait()
    parts = [split(x_ref[pl.ds(d, SEGMENTS, stride=OWN_DETS), :]) for d in range(OWN_DETS)]
    outer = (outer_ref[0], outer_ref[1])
    samples = tuple(jnp.concatenate([part[i] for part in parts], axis=1) for i in range(2))
    section = dot3(outer, samples, NN)
    for copy in copies[3:8]:
        copy.wait()
    inner = (inner_ref[0], inner_ref[1])
    cos, sin, log_fold = factors_ref[0], factors_ref[1], factors_ref[2]
    top = lax.broadcasted_iota(jnp.int32, (8, SEGLEN), 0) == 0
    stacked = []
    for d in range(OWN_DETS):
        cut = slice(SEGLEN * d, SEGLEN * (d + 1))
        real, imag = section[:HALF, cut], section[HALF:, cut]
        real = jnp.concatenate([real, jnp.where(top, imag[:8], 0.0)], axis=0)
        imag = jnp.concatenate([jnp.where(top, 0.0, imag[:8]), imag[8:], jnp.zeros((8, SEGLEN), f32)], axis=0)
        stacked.append(jnp.concatenate([real * cos + imag * sin, imag * cos - real * sin], axis=1))
    spectrum = dot3(split(jnp.concatenate(stacked, axis=0)), inner, NN)
    row = lax.broadcasted_iota(jnp.int32, (ROWS, SEGLEN), 0)
    zero_freq = (row == 0) & (lax.broadcasted_iota(jnp.int32, (ROWS, SEGLEN), 1) == 0)
    times = jnp.where((row == 0) | (row == HALF), 1.0 / SAMPLES, 2.0 / SAMPLES).astype(f32)
    shaped = []
    for d in range(OWN_DETS):
        log_knee = jnp.log(jnp.full((1, SEGLEN), knee_ref[d], f32))
        slope = slope_ref[d]
        level = jnp.full((1, SEGLEN), level_ref[d], f32)
        ratio = jnp.exp(slope * (log_knee - log_fold))
        weight = jnp.where(zero_freq, 0.0, times / ((1.0 + ratio) * (level * level)))
        part = spectrum[ROWS * d : ROWS * (d + 1)]
        shaped.append(part * jnp.concatenate([weight, weight], axis=1))
    back = dot3(split(jnp.concatenate(shaped, axis=0)), inner, NT)
    turned = []
    for d in range(OWN_DETS):
        part = back[ROWS * d : ROWS * (d + 1)]
        real, imag = part[:, :SEGLEN], part[:, SEGLEN:]
        turn_re = real * cos - imag * sin
        turn_im = imag * cos + real * sin
        first = jnp.where(top, jnp.broadcast_to(turn_re[HALF : HALF + 1], (8, SEGLEN)), turn_im[:8])
        turned.append(jnp.concatenate([turn_re[:HALF], first, turn_im[8:HALF]], axis=0))
    copies[8].wait()
    result = dot3((back_ref[0], back_ref[1]), split(jnp.concatenate(turned, axis=1)), NN)
    for plane in range(PLANES):
        for core in range(2):
            start = held_at(plane, core)
            for d in range(OWN_DETS):
                row = (PLANE * plane + core) * OWN_DETS + d
                out_ref[pl.ds(row, GROUP, stride=2 * OWN_DETS), :] = result[
                    start : start + GROUP, SEGLEN * d : SEGLEN * (d + 1)
                ]


def project_kernel(data_ref, templates_ref, clean_ref, power_ref):
    data = data_ref[...].T
    pattern = split(templates_ref[...])
    amplitudes = dot3(split(data), pattern, NN)
    cleaned = data - dot3(split(amplitudes), pattern, NT)
    clean_ref[...] = cleaned
    power = jnp.sum(cleaned * cleaned, axis=0, keepdims=True)
    power = jnp.concatenate([power[:, SEGLEN * k : SEGLEN * (k + 1)] for k in range(8)], axis=0)
    for member in range(PLANE):
        power_ref[member] = power


def slot_kernel(segment_ref, index_ref, slot_ref, hot_ref):
    segment = segment_ref[0]
    pick = lax.broadcasted_iota(jnp.int32, (8, SEGMENTS), 1) == segment
    index = index_ref[...].astype(f32).astype(bf16)
    seen = lax.dot_general(
        jnp.where(pick, 1.0, 0.0).astype(bf16), index, (NT, ((), ())), preferred_element_type=f32
    )
    block = lax.broadcasted_iota(jnp.int32, (BLOCKS, DETS), 0)
    hot = jnp.where(jnp.broadcast_to(seen[0:1].astype(jnp.int32), (BLOCKS, DETS)) == block, 1.0, 0.0).astype(bf16)
    table = jnp.broadcast_to(slot_ref[...].astype(f32).astype(bf16), (8, BLOCKS))
    slot = lax.dot_general(table, hot, (NN, ((), ())), preferred_element_type=f32)
    row = ((block >> 3) & 7) * 32 + (block >> 6) * 8 + (block & 7)
    hot_ref[...] = jnp.where(
        jnp.broadcast_to(slot[0:1].astype(jnp.int32), (BLOCKS, DETS)) == row, 1.0, 0.0
    ).astype(bf16)


def halo_kernel(gathered_ref, weight_ref, beyond_ref, own_ref, message_ref):
    own = jnp.full((8, SEGLEN), EPS, f32)
    message = jnp.zeros((8, SEGLEN), f32)
    for member in range(PLANE):
        power = gathered_ref[member]
        own = own + weight_ref[member] * power
        message = message + beyond_ref[member] * power
    own_ref[...] = own
    message_ref[...] = message


def bin_kernel(clean_ref, own_ref, share_ref, message_ref, hot_ref, map_ref):
    inverse = 1.0 / (own_ref[...] + share_ref[...] * message_ref[...])
    values = jnp.concatenate(
        [clean_ref[:, SEGLEN * k : SEGLEN * (k + 1)] * inverse[k : k + 1] for k in range(8)], axis=1
    )
    high, low = split(values)
    hot = hot_ref[...]
    map_ref[...] = lax.dot_general(hot, high, (NT, ((), ())), preferred_element_type=f32) + lax.dot_general(
        hot, low, (NT, ((), ())), preferred_element_type=f32
    )


def fold_kernel(parts_ref, out_ref):
    total = parts_ref[0]
    for i in range(1, parts_ref.shape[0]):
        total = total + parts_ref[i]
    total = total * MAP_SCALE
    for i in range(out_ref.shape[0]):
        out_ref[i] = total


VMEM = pl.BlockSpec(memory_space=pltpu.VMEM)
SMEM = pl.BlockSpec(memory_space=pltpu.SMEM)
HBM = pl.BlockSpec(memory_space=pltpu.HBM)


def call(kernel, specs, outs, name, scratch=()):
    shapes = [pltpu.VMEM(shape, dtype) for shape, dtype in outs]
    return pl.pallas_call(
        kernel,
        out_shape=shapes if len(shapes) > 1 else shapes[0],
        in_specs=specs,
        out_specs=[VMEM] * len(shapes) if len(shapes) > 1 else VMEM,
        scratch_shapes=list(scratch),
        compiler_params=pltpu.CompilerParams(vmem_limit_bytes=16 * 1024 * 1024),
        name=name,
    )


def interval_groups():
    groups = []
    for k in range(PLANES):
        early = [PLANE * ((k - 1) % PLANES) + 2 * m + 1 for m in range(GROUP)]
        groups.append(early + [PLANE * k + 2 * m for m in range(GROUP)])
    return groups


def local(timelines, knee_freq, noise_slope, noise_level, templates, interval_bounds, block_index, block_slot):
    core = lax.axis_index("c")
    group = lax.rem(lax.axis_index("z") + core, PLANES)
    segment = (PLANE * group + GROUP * (1 - core) + lax.axis_index(("y", "x"))).astype(jnp.int32).reshape(1)
    rows = timelines.reshape(OWN_DETS, SEGMENTS, SEGLEN).transpose(1, 0, 2).reshape(DETS, SEGLEN)
    scratch = [pltpu.SMEM((INTERVALS + 1,), jnp.int32)] + [pltpu.SMEM((OWN_DETS,), f32)] * 3 + [
        pltpu.VMEM((DETS, SEGLEN), f32),
        pltpu.VMEM((2, SEGMENTS, SEGMENTS), bf16),
        pltpu.VMEM((2, SEGMENTS, SEGMENTS), bf16),
        pltpu.VMEM((2, SEGMENTS, SEGMENTS), bf16),
        pltpu.VMEM((3, ROWS, SEGLEN), f32),
        pltpu.SemaphoreType.DMA((9,)),
    ]
    stored = [interval_bounds, knee_freq, noise_slope, noise_level, rows, *[jnp.asarray(t) for t in tables()]]
    line, lines = ((8, SEGLEN), f32), ((PLANE, 8, SEGLEN), f32)
    weighted, inside, outside, share = call(
        weight_kernel, [HBM] * 7, [((DETS, SEGLEN), f32), lines, lines, line], "weight", scratch
    )(*[pltpu.with_memory_space_constraint(array, pltpu.HBM) for array in stored])
    data = lax.all_to_all(
        weighted.reshape(SEGMENTS, OWN_DETS, SEGLEN), ALL, split_axis=0, concat_axis=0, tiled=True
    ).reshape(DETS, SEGLEN)
    cleaned, power = call(project_kernel, [VMEM] * 2, [((SEGLEN, DETS), f32), lines], "project")(data, templates)
    gathered = lax.all_to_all(
        power, ALL, split_axis=0, concat_axis=0, axis_index_groups=interval_groups(), tiled=True
    )
    own, message = call(halo_kernel, [VMEM] * 3, [line] * 2, "halo")(gathered, inside, outside)
    message, block_index = lax.optimization_barrier((message, block_index))
    beyond = lax.ppermute(message, "c", [(0, 1), (1, 0)])
    hot = call(slot_kernel, [SMEM] + [VMEM] * 2, [((BLOCKS, DETS), bf16)], "slots")(
        segment, block_index, block_slot.reshape(1, BLOCKS)
    )
    partial = call(bin_kernel, [VMEM] * 5, [((BLOCKS, SEGLEN), f32)], "bin")(cleaned, own, share, beyond, hot)
    spread = lax.all_to_all(
        partial.reshape(32, 8, SEGLEN), ("y", "x", "c"), split_axis=0, concat_axis=0, tiled=True
    )
    copies = call(fold_kernel, [VMEM], [((32, 8, SEGLEN), f32)], "fold")(spread)
    sums = lax.all_to_all(copies, ("z", "y"), split_axis=0, concat_axis=0, tiled=True)
    return jnp.sum(sums.reshape(8, 32, SEGLEN), axis=0)


def solution(mesh):
    whole = Mesh(mesh.devices.reshape(8, 4, 4, 2), ALL)
    return jax.shard_map(
        local,
        mesh=whole,
        in_specs=(P(ALL, None), P(ALL), P(ALL), P(ALL), P(), P(), P(), P()),
        out_specs=P(("x", "c"), None),
        check_vma=False,
    )
```

```python
import math

import jax
import jax.numpy as jnp
import numpy as np
from jax import lax
from jax.experimental import pallas as pl
from jax.experimental.pallas import tpu as pltpu
from jax.sharding import Mesh, PartitionSpec as P

DETS = 1024
SAMPLES = 32768
TEMPLATES = 512
SEGLEN = 128
SEGMENTS = 256
BLOCKS = 256
INTERVALS = 32
EPS = 1e-06
OWN_DETS = 4
HALF = SEGMENTS // 2
ROWS = HALF + 8
GROUP = 16
PLANE = 2 * GROUP
MAP_SCALE = 1.0 / math.sqrt(DETS * SAMPLES // (SEGLEN * BLOCKS))
ALL = ("z", "y", "x", "c")
PLANES = 8
bf16 = jnp.bfloat16
f32 = jnp.float32


def split_np(table):
    parts = []
    rest = np.asarray(table, np.float64)
    for _ in range(3):
        parts.append(rest.astype(np.float32).astype(jnp.bfloat16))
        rest = rest - parts[-1].astype(np.float64)
    return parts


def tables():
    k = np.arange(HALF)
    c = np.arange(SEGMENTS)
    angle = 2.0 * np.pi * ((k[:, None] * c[None, :]) % SEGMENTS) / SEGMENTS
    outer = np.concatenate([np.cos(angle), -np.sin(angle)], axis=0)
    outer[HALF] = 1.0 - 2.0 * (c % 2)
    p = np.arange(SEGLEN)
    angle = 2.0 * np.pi * ((p[:, None] * p[None, :]) % SEGLEN) / SEGLEN
    inner = np.block([[np.cos(angle), -np.sin(angle)], [np.sin(angle), np.cos(angle)]])
    row = np.arange(ROWS)
    angle = 2.0 * np.pi * (row[:, None] * p[None, :]) / SAMPLES
    freq = row[:, None] + SEGMENTS * p[None, :]
    fold = np.minimum(freq, SAMPLES - freq)
    log_fold = np.where(fold > 0, np.log(np.maximum(fold, 1)), 0.0)
    return (
        np.stack([*split_np(outer), *split_np(inner), *split_np(outer.T)]),
        np.stack([np.cos(angle), np.sin(angle), log_fold]).astype(np.float32),
    )


def split(value):
    high = value.astype(bf16)
    rest = value - high.astype(f32)
    middle = rest.astype(bf16)
    return high, middle, (rest - middle.astype(f32)).astype(bf16)


def dot6(a, b, dims):
    rows = a[0].shape[0]
    total = None
    for k in (2, 1, 0):
        left = jnp.concatenate(a[: 3 - k], axis=0) if k < 2 else a[0]
        product = lax.dot_general(left, b[k], (dims, ((), ())), preferred_element_type=f32)
        for i in reversed(range(3 - k)):
            part = product[rows * i : rows * (i + 1)]
            total = part if total is None else total + part
    return total


NN = ((1,), (0,))
NT = ((1,), (1,))


def held_at(plane, core):
    return PLANE * ((plane + core) % PLANES) + GROUP * (1 - core)


def interval_of(bounds_ref, segment):
    at = segment * SEGLEN
    first = jnp.int32(0)
    end = jnp.int32(SAMPLES)
    for t in range(1, INTERVALS):
        bound = bounds_ref[t]
        first = jnp.where(bound <= at, jnp.maximum(first, bound), first)
        end = jnp.where(bound > at, jnp.minimum(end, bound), end)
    return first // SEGLEN, end // SEGLEN


def member_weights(bounds_ref, inside_ref, outside_ref, share_ref):
    core = lax.axis_index("c")
    base = PLANE * lax.rem(lax.axis_index("z") + core, PLANES)
    segment = base + GROUP * (1 - core) + 4 * lax.axis_index("y") + lax.axis_index("x")
    late = core == 0
    first, end = interval_of(bounds_ref, segment)
    part = 1.0 / jnp.full((8, SEGLEN), (end - first) * SEGLEN, jnp.int32).astype(f32)
    share_ref[...] = jnp.where(jnp.where(late, end > base + PLANE, first < base), part, 0.0)
    next_first, next_end = interval_of(bounds_ref, jnp.where(late, base + PLANE, base - 1))
    edge = jnp.where(late, base + PLANE == SEGMENTS, base == 0)
    next_first = jnp.where(edge, next_end, next_first)
    for member in range(PLANE):
        at = base + member
        inside_ref[member] = jnp.where((at >= first) & (at < end), part, 0.0)
        outside_ref[member] = jnp.full((8, SEGLEN), jnp.where((at >= next_first) & (at < next_end), 1.0, 0.0), f32)


def weight_kernel(
    bounds_hbm, knee_hbm, slope_hbm, level_hbm, x_hbm, tables_hbm, factors_hbm,
    out_ref, inside_ref, outside_ref, share_ref,
    bounds_ref, knee_ref, slope_ref, level_ref, x_ref, outer_ref, inner_ref, back_ref, factors_ref, sems,
):
    pairs = [
        (bounds_hbm, bounds_ref),
        (x_hbm, x_ref),
        (tables_hbm.at[pl.ds(0, 3)], outer_ref),
        (factors_hbm, factors_ref),
        (tables_hbm.at[pl.ds(3, 3)], inner_ref),
        (knee_hbm, knee_ref),
        (slope_hbm, slope_ref),
        (level_hbm, level_ref),
        (tables_hbm.at[pl.ds(6, 3)], back_ref),
    ]
    copies = [pltpu.make_async_copy(src, dst, sems.at[i]) for i, (src, dst) in enumerate(pairs)]
    for copy in copies:
        copy.start()
    copies[0].wait()
    member_weights(bounds_ref, inside_ref, outside_ref, share_ref)
    copies[1].wait()
    copies[2].wait()
    parts = [split(x_ref[pl.ds(d, SEGMENTS, stride=OWN_DETS), :]) for d in range(OWN_DETS)]
    outer = (outer_ref[0], outer_ref[1], outer_ref[2])
    samples = tuple(jnp.concatenate([part[i] for part in parts], axis=1) for i in range(3))
    section = dot6(outer, samples, NN)
    for copy in copies[3:8]:
        copy.wait()
    inner = (inner_ref[0], inner_ref[1], inner_ref[2])
    cos, sin, log_fold = factors_ref[0], factors_ref[1], factors_ref[2]
    top = lax.broadcasted_iota(jnp.int32, (8, SEGLEN), 0) == 0
    stacked = []
    for d in range(OWN_DETS):
        cut = slice(SEGLEN * d, SEGLEN * (d + 1))
        real, imag = section[:HALF, cut], section[HALF:, cut]
        real = jnp.concatenate([real, jnp.where(top, imag[:8], 0.0)], axis=0)
        imag = jnp.concatenate([jnp.where(top, 0.0, imag[:8]), imag[8:], jnp.zeros((8, SEGLEN), f32)], axis=0)
        stacked.append(jnp.concatenate([real * cos + imag * sin, imag * cos - real * sin], axis=1))
    spectrum = dot6(split(jnp.concatenate(stacked, axis=0)), inner, NN)
    row = lax.broadcasted_iota(jnp.int32, (ROWS, SEGLEN), 0)
    zero_freq = (row == 0) & (lax.broadcasted_iota(jnp.int32, (ROWS, SEGLEN), 1) == 0)
    times = jnp.where((row == 0) | (row == HALF), 1.0 / SAMPLES, 2.0 / SAMPLES).astype(f32)
    shaped = []
    for d in range(OWN_DETS):
        log_knee = jnp.log(jnp.full((1, SEGLEN), knee_ref[d], f32))
        slope = slope_ref[d]
        level = jnp.full((1, SEGLEN), level_ref[d], f32)
        ratio = jnp.exp(slope * (log_knee - log_fold))
        weight = jnp.where(zero_freq, 0.0, times / ((1.0 + ratio) * (level * level)))
        part = spectrum[ROWS * d : ROWS * (d + 1)]
        shaped.append(part * jnp.concatenate([weight, weight], axis=1))
    back = dot6(split(jnp.concatenate(shaped, axis=0)), inner, NT)
    turned = []
    for d in range(OWN_DETS):
        part = back[ROWS * d : ROWS * (d + 1)]
        real, imag = part[:, :SEGLEN], part[:, SEGLEN:]
        turn_re = real * cos - imag * sin
        turn_im = imag * cos + real * sin
        first = jnp.where(top, jnp.broadcast_to(turn_re[HALF : HALF + 1], (8, SEGLEN)), turn_im[:8])
        turned.append(jnp.concatenate([turn_re[:HALF], first, turn_im[8:HALF]], axis=0))
    copies[8].wait()
    result = dot6((back_ref[0], back_ref[1], back_ref[2]), split(jnp.concatenate(turned, axis=1)), NN)
    for plane in range(PLANES):
        for core in range(2):
            start = held_at(plane, core)
            for d in range(OWN_DETS):
                row = (PLANE * plane + core) * OWN_DETS + d
                out_ref[pl.ds(row, GROUP, stride=2 * OWN_DETS), :] = result[
                    start : start + GROUP, SEGLEN * d : SEGLEN * (d + 1)
                ]


def project_kernel(data_ref, templates_ref, clean_ref, power_ref):
    data = data_ref[...].T
    pattern = split(templates_ref[...])
    amplitudes = dot6(split(data), pattern, NN)
    cleaned = data - dot6(split(amplitudes), pattern, NT)
    clean_ref[...] = cleaned
    power = jnp.sum(cleaned * cleaned, axis=0, keepdims=True)
    power = jnp.concatenate([power[:, SEGLEN * k : SEGLEN * (k + 1)] for k in range(8)], axis=0)
    for member in range(PLANE):
        power_ref[member] = power


def slot_kernel(segment_ref, index_ref, slot_ref, hot_ref):
    segment = segment_ref[0]
    pick = lax.broadcasted_iota(jnp.int32, (8, SEGMENTS), 1) == segment
    index = index_ref[...].astype(f32).astype(bf16)
    seen = lax.dot_general(
        jnp.where(pick, 1.0, 0.0).astype(bf16), index, (NT, ((), ())), preferred_element_type=f32
    )
    block = lax.broadcasted_iota(jnp.int32, (BLOCKS, DETS), 0)
    hot = jnp.where(jnp.broadcast_to(seen[0:1].astype(jnp.int32), (BLOCKS, DETS)) == block, 1.0, 0.0).astype(bf16)
    table = jnp.broadcast_to(slot_ref[...].astype(f32).astype(bf16), (8, BLOCKS))
    slot = lax.dot_general(table, hot, (NN, ((), ())), preferred_element_type=f32)
    row = ((block >> 3) & 7) * 32 + (block >> 6) * 8 + (block & 7)
    hot_ref[...] = jnp.where(
        jnp.broadcast_to(slot[0:1].astype(jnp.int32), (BLOCKS, DETS)) == row, 1.0, 0.0
    ).astype(bf16)


def halo_kernel(gathered_ref, weight_ref, beyond_ref, own_ref, message_ref):
    own = jnp.full((8, SEGLEN), EPS, f32)
    message = jnp.zeros((8, SEGLEN), f32)
    for member in range(PLANE):
        power = gathered_ref[member]
        own = own + weight_ref[member] * power
        message = message + beyond_ref[member] * power
    own_ref[...] = own
    message_ref[...] = message


def bin_kernel(clean_ref, own_ref, share_ref, message_ref, hot_ref, map_ref):
    inverse = 1.0 / (own_ref[...] + share_ref[...] * message_ref[...])
    values = jnp.concatenate(
        [clean_ref[:, SEGLEN * k : SEGLEN * (k + 1)] * inverse[k : k + 1] for k in range(8)], axis=1
    )
    parts = lax.dot_general(
        hot_ref[...], jnp.concatenate(split(values), axis=0), (NT, ((), ())), preferred_element_type=f32
    )
    map_ref[...] = parts[:, :SEGLEN] + (parts[:, SEGLEN : 2 * SEGLEN] + parts[:, 2 * SEGLEN :])


def fold_kernel(parts_ref, out_ref):
    total = parts_ref[0]
    for i in range(1, parts_ref.shape[0]):
        total = total + parts_ref[i]
    total = total * MAP_SCALE
    for i in range(out_ref.shape[0]):
        out_ref[i] = total


VMEM = pl.BlockSpec(memory_space=pltpu.VMEM)
SMEM = pl.BlockSpec(memory_space=pltpu.SMEM)
HBM = pl.BlockSpec(memory_space=pltpu.HBM)


def call(kernel, specs, outs, name, scratch=()):
    shapes = [pltpu.VMEM(shape, dtype) for shape, dtype in outs]
    return pl.pallas_call(
        kernel,
        out_shape=shapes if len(shapes) > 1 else shapes[0],
        in_specs=specs,
        out_specs=[VMEM] * len(shapes) if len(shapes) > 1 else VMEM,
        scratch_shapes=list(scratch),
        compiler_params=pltpu.CompilerParams(vmem_limit_bytes=16 * 1024 * 1024),
        name=name,
    )


def interval_groups():
    groups = []
    for k in range(PLANES):
        early = [PLANE * ((k - 1) % PLANES) + 2 * m + 1 for m in range(GROUP)]
        groups.append(early + [PLANE * k + 2 * m for m in range(GROUP)])
    return groups


def local(timelines, knee_freq, noise_slope, noise_level, templates, interval_bounds, block_index, block_slot):
    core = lax.axis_index("c")
    group = lax.rem(lax.axis_index("z") + core, PLANES)
    segment = (PLANE * group + GROUP * (1 - core) + lax.axis_index(("y", "x"))).astype(jnp.int32).reshape(1)
    rows = timelines.reshape(OWN_DETS, SEGMENTS, SEGLEN).transpose(1, 0, 2).reshape(DETS, SEGLEN)
    scratch = [pltpu.SMEM((INTERVALS + 1,), jnp.int32)] + [pltpu.SMEM((OWN_DETS,), f32)] * 3 + [
        pltpu.VMEM((DETS, SEGLEN), f32),
        pltpu.VMEM((3, SEGMENTS, SEGMENTS), bf16),
        pltpu.VMEM((3, SEGMENTS, SEGMENTS), bf16),
        pltpu.VMEM((3, SEGMENTS, SEGMENTS), bf16),
        pltpu.VMEM((3, ROWS, SEGLEN), f32),
        pltpu.SemaphoreType.DMA((9,)),
    ]
    stored = [interval_bounds, knee_freq, noise_slope, noise_level, rows, *[jnp.asarray(t) for t in tables()]]
    line, lines = ((8, SEGLEN), f32), ((PLANE, 8, SEGLEN), f32)
    weighted, inside, outside, share = call(
        weight_kernel, [HBM] * 7, [((DETS, SEGLEN), f32), lines, lines, line], "weight", scratch
    )(*[pltpu.with_memory_space_constraint(array, pltpu.HBM) for array in stored])
    data = lax.all_to_all(
        weighted.reshape(SEGMENTS, OWN_DETS, SEGLEN), ALL, split_axis=0, concat_axis=0, tiled=True
    ).reshape(DETS, SEGLEN)
    cleaned, power = call(project_kernel, [VMEM] * 2, [((SEGLEN, DETS), f32), lines], "project")(data, templates)
    gathered = lax.all_to_all(
        power, ALL, split_axis=0, concat_axis=0, axis_index_groups=interval_groups(), tiled=True
    )
    own, message = call(halo_kernel, [VMEM] * 3, [line] * 2, "halo")(gathered, inside, outside)
    message, block_index = lax.optimization_barrier((message, block_index))
    beyond = lax.ppermute(message, "c", [(0, 1), (1, 0)])
    hot = call(slot_kernel, [SMEM] + [VMEM] * 2, [((BLOCKS, DETS), bf16)], "slots")(
        segment, block_index, block_slot.reshape(1, BLOCKS)
    )
    partial = call(bin_kernel, [VMEM] * 5, [((BLOCKS, SEGLEN), f32)], "bin")(cleaned, own, share, beyond, hot)
    spread = lax.all_to_all(
        partial.reshape(32, 8, SEGLEN), ("y", "x", "c"), split_axis=0, concat_axis=0, tiled=True
    )
    copies = call(fold_kernel, [VMEM], [((32, 8, SEGLEN), f32)], "fold")(spread)
    sums = lax.all_to_all(copies, ("z", "y"), split_axis=0, concat_axis=0, tiled=True)
    return jnp.sum(sums.reshape(8, 32, SEGLEN), axis=0)


def solution(mesh):
    whole = Mesh(mesh.devices.reshape(8, 4, 4, 2), ALL)
    return jax.shard_map(
        local,
        mesh=whole,
        in_specs=(P(ALL, None), P(ALL), P(ALL), P(ALL), P(), P(), P(), P()),
        out_specs=P(("x", "c"), None),
        check_vma=False,
    )
```

```python
import math

import jax
import jax.numpy as jnp
import numpy as np
from jax import lax
from jax.experimental import pallas as pl
from jax.experimental.pallas import tpu as pltpu
from jax.sharding import Mesh, PartitionSpec as P

DETS = 1024
SAMPLES = 32768
TEMPLATES = 512
SEGLEN = 128
SEGMENTS = 256
BLOCKS = 256
INTERVALS = 32
EPS = 1e-06
OWN_DETS = 4
HALF = SEGMENTS // 2
ROWS = HALF + 8
GROUP = 16
PLANE = 2 * GROUP
MAP_SCALE = 1.0 / math.sqrt(DETS * SAMPLES // (SEGLEN * BLOCKS))
ALL = ("z", "y", "x", "c")
PLANES = 8
bf16 = jnp.bfloat16
f32 = jnp.float32


def split_np(table):
    high = np.asarray(table, np.float32).astype(jnp.bfloat16)
    low = (table - high.astype(np.float64)).astype(np.float32).astype(jnp.bfloat16)
    return high, low


def tables():
    k = np.arange(HALF)
    c = np.arange(SEGMENTS)
    angle = 2.0 * np.pi * ((k[:, None] * c[None, :]) % SEGMENTS) / SEGMENTS
    outer = np.concatenate([np.cos(angle), -np.sin(angle)], axis=0)
    outer[HALF] = 1.0 - 2.0 * (c % 2)
    p = np.arange(SEGLEN)
    angle = 2.0 * np.pi * ((p[:, None] * p[None, :]) % SEGLEN) / SEGLEN
    inner = np.block([[np.cos(angle), -np.sin(angle)], [np.sin(angle), np.cos(angle)]])
    row = np.arange(ROWS)
    angle = 2.0 * np.pi * (row[:, None] * p[None, :]) / SAMPLES
    freq = row[:, None] + SEGMENTS * p[None, :]
    fold = np.minimum(freq, SAMPLES - freq)
    log_fold = np.where(fold > 0, np.log(np.maximum(fold, 1)), 0.0)
    return (
        np.stack([*split_np(outer), *split_np(inner), *split_np(outer.T)]),
        np.stack([np.cos(angle), np.sin(angle), log_fold]).astype(np.float32),
    )


def split(value):
    high = value.astype(bf16)
    return high, (value - high.astype(f32)).astype(bf16)


def dot3(a, b, dims):
    def one(x, y):
        return lax.dot_general(x, y, (dims, ((), ())), preferred_element_type=f32)

    rows = a[0].shape[0]
    both = one(jnp.concatenate(a, axis=0), b[0])
    return both[:rows] + (both[rows:] + one(a[0], b[1]))


NN = ((1,), (0,))
NT = ((1,), (1,))


def held_at(plane, core):
    return PLANE * ((plane + core) % PLANES) + GROUP * (1 - core)


def interval_of(bounds_ref, segment):
    at = segment * SEGLEN
    first = jnp.int32(0)
    end = jnp.int32(SAMPLES)
    for t in range(1, INTERVALS):
        bound = bounds_ref[t]
        first = jnp.where(bound <= at, jnp.maximum(first, bound), first)
        end = jnp.where(bound > at, jnp.minimum(end, bound), end)
    return first // SEGLEN, end // SEGLEN


def member_weights(bounds_ref, inside_ref, outside_ref, share_ref):
    core = lax.axis_index("c")
    base = PLANE * lax.rem(lax.axis_index("z") + core, PLANES)
    segment = base + GROUP * (1 - core) + 4 * lax.axis_index("y") + lax.axis_index("x")
    late = core == 0
    first, end = interval_of(bounds_ref, segment)
    part = 1.0 / jnp.full((8, SEGLEN), (end - first) * SEGLEN, jnp.int32).astype(f32)
    share_ref[...] = jnp.where(jnp.where(late, end > base + PLANE, first < base), part, 0.0)
    next_first, next_end = interval_of(bounds_ref, jnp.where(late, base + PLANE, base - 1))
    edge = jnp.where(late, base + PLANE == SEGMENTS, base == 0)
    next_first = jnp.where(edge, next_end, next_first)
    for member in range(PLANE):
        at = base + member
        inside_ref[member] = jnp.where((at >= first) & (at < end), part, 0.0)
        outside_ref[member] = jnp.full((8, SEGLEN), jnp.where((at >= next_first) & (at < next_end), 1.0, 0.0), f32)


def weight_kernel(
    bounds_hbm, knee_hbm, slope_hbm, level_hbm, x_hbm, tables_hbm, factors_hbm,
    out_ref, inside_ref, outside_ref, share_ref,
    bounds_ref, knee_ref, slope_ref, level_ref, x_ref, outer_ref, inner_ref, back_ref, factors_ref, sems,
):
    pairs = [
        (bounds_hbm, bounds_ref),
        (x_hbm, x_ref),
        (tables_hbm.at[pl.ds(0, 2)], outer_ref),
        (factors_hbm, factors_ref),
        (tables_hbm.at[pl.ds(2, 2)], inner_ref),
        (knee_hbm, knee_ref),
        (slope_hbm, slope_ref),
        (level_hbm, level_ref),
        (tables_hbm.at[pl.ds(4, 2)], back_ref),
    ]
    copies = [pltpu.make_async_copy(src, dst, sems.at[i]) for i, (src, dst) in enumerate(pairs)]
    for copy in copies:
        copy.start()
    copies[0].wait()
    member_weights(bounds_ref, inside_ref, outside_ref, share_ref)
    copies[1].wait()
    copies[2].wait()
    parts = [split(x_ref[pl.ds(d, SEGMENTS, stride=OWN_DETS), :]) for d in range(OWN_DETS)]
    outer = (outer_ref[0], outer_ref[1])
    samples = tuple(jnp.concatenate([part[i] for part in parts], axis=1) for i in range(2))
    section = dot3(outer, samples, NN)
    for copy in copies[3:8]:
        copy.wait()
    inner = (inner_ref[0], inner_ref[1])
    cos, sin, log_fold = factors_ref[0], factors_ref[1], factors_ref[2]
    top = lax.broadcasted_iota(jnp.int32, (8, SEGLEN), 0) == 0
    stacked = []
    for d in range(OWN_DETS):
        cut = slice(SEGLEN * d, SEGLEN * (d + 1))
        real, imag = section[:HALF, cut], section[HALF:, cut]
        real = jnp.concatenate([real, jnp.where(top, imag[:8], 0.0)], axis=0)
        imag = jnp.concatenate([jnp.where(top, 0.0, imag[:8]), imag[8:], jnp.zeros((8, SEGLEN), f32)], axis=0)
        stacked.append(jnp.concatenate([real * cos + imag * sin, imag * cos - real * sin], axis=1))
    spectrum = dot3(split(jnp.concatenate(stacked, axis=0)), inner, NN)
    row = lax.broadcasted_iota(jnp.int32, (ROWS, SEGLEN), 0)
    zero_freq = (row == 0) & (lax.broadcasted_iota(jnp.int32, (ROWS, SEGLEN), 1) == 0)
    times = jnp.where((row == 0) | (row == HALF), 1.0 / SAMPLES, 2.0 / SAMPLES).astype(f32)
    shaped = []
    for d in range(OWN_DETS):
        log_knee = jnp.log(jnp.full((1, SEGLEN), knee_ref[d], f32))
        slope = slope_ref[d]
        level = jnp.full((1, SEGLEN), level_ref[d], f32)
        ratio = jnp.exp(slope * (log_knee - log_fold))
        weight = jnp.where(zero_freq, 0.0, times / ((1.0 + ratio) * (level * level)))
        part = spectrum[ROWS * d : ROWS * (d + 1)]
        shaped.append(part * jnp.concatenate([weight, weight], axis=1))
    back = dot3(split(jnp.concatenate(shaped, axis=0)), inner, NT)
    turned = []
    for d in range(OWN_DETS):
        part = back[ROWS * d : ROWS * (d + 1)]
        real, imag = part[:, :SEGLEN], part[:, SEGLEN:]
        turn_re = real * cos - imag * sin
        turn_im = imag * cos + real * sin
        first = jnp.where(top, jnp.broadcast_to(turn_re[HALF : HALF + 1], (8, SEGLEN)), turn_im[:8])
        turned.append(jnp.concatenate([turn_re[:HALF], first, turn_im[8:HALF]], axis=0))
    copies[8].wait()
    result = dot3((back_ref[0], back_ref[1]), split(jnp.concatenate(turned, axis=1)), NN)
    for plane in range(PLANES):
        for core in range(2):
            start = held_at(plane, core)
            for d in range(OWN_DETS):
                row = (PLANE * plane + core) * OWN_DETS + d
                out_ref[pl.ds(row, GROUP, stride=2 * OWN_DETS), :] = result[
                    start : start + GROUP, SEGLEN * d : SEGLEN * (d + 1)
                ]


def project_kernel(data_ref, templates_ref, clean_ref, power_ref):
    data = data_ref[...].T
    pattern = split(templates_ref[...])
    amplitudes = dot3(split(data), pattern, NN)
    cleaned = data - dot3(split(amplitudes), pattern, NT)
    clean_ref[...] = cleaned
    power = jnp.sum(cleaned * cleaned, axis=0, keepdims=True)
    power = jnp.concatenate([power[:, SEGLEN * k : SEGLEN * (k + 1)] for k in range(8)], axis=0)
    for member in range(PLANE):
        power_ref[member] = power


def slot_kernel(segment_ref, index_ref, slot_ref, hot_ref):
    segment = segment_ref[0]
    pick = lax.broadcasted_iota(jnp.int32, (8, SEGMENTS), 1) == segment
    index = index_ref[...].astype(f32).astype(bf16)
    seen = lax.dot_general(
        jnp.where(pick, 1.0, 0.0).astype(bf16), index, (NT, ((), ())), preferred_element_type=f32
    )
    block = lax.broadcasted_iota(jnp.int32, (BLOCKS, DETS), 0)
    hot = jnp.where(jnp.broadcast_to(seen[0:1].astype(jnp.int32), (BLOCKS, DETS)) == block, 1.0, 0.0).astype(bf16)
    table = jnp.broadcast_to(slot_ref[...].astype(f32).astype(bf16), (8, BLOCKS))
    slot = lax.dot_general(table, hot, (NN, ((), ())), preferred_element_type=f32)
    row = ((block >> 3) & 7) * 32 + (block >> 6) * 8 + (block & 7)
    hot_ref[...] = jnp.where(
        jnp.broadcast_to(slot[0:1].astype(jnp.int32), (BLOCKS, DETS)) == row, 1.0, 0.0
    ).astype(bf16)


def halo_kernel(gathered_ref, weight_ref, beyond_ref, own_ref, message_ref):
    own = jnp.full((8, SEGLEN), EPS, f32)
    message = jnp.zeros((8, SEGLEN), f32)
    for member in range(PLANE):
        power = gathered_ref[member]
        own = own + weight_ref[member] * power
        message = message + beyond_ref[member] * power
    own_ref[...] = own
    message_ref[...] = message


def bin_kernel(clean_ref, own_ref, share_ref, message_ref, hot_ref, map_ref):
    inverse = 1.0 / (own_ref[...] + share_ref[...] * message_ref[...])
    values = jnp.concatenate(
        [clean_ref[:, SEGLEN * k : SEGLEN * (k + 1)] * inverse[k : k + 1] for k in range(8)], axis=1
    )
    both = lax.dot_general(
        hot_ref[...], jnp.concatenate(split(values), axis=0), (NT, ((), ())), preferred_element_type=f32
    )
    map_ref[...] = both[:, :SEGLEN] + both[:, SEGLEN:]


def fold_kernel(parts_ref, out_ref):
    total = parts_ref[0]
    for i in range(1, parts_ref.shape[0]):
        total = total + parts_ref[i]
    total = total * MAP_SCALE
    for i in range(out_ref.shape[0]):
        out_ref[i] = total


VMEM = pl.BlockSpec(memory_space=pltpu.VMEM)
SMEM = pl.BlockSpec(memory_space=pltpu.SMEM)
HBM = pl.BlockSpec(memory_space=pltpu.HBM)


def call(kernel, specs, outs, name, scratch=()):
    shapes = [pltpu.VMEM(shape, dtype) for shape, dtype in outs]
    return pl.pallas_call(
        kernel,
        out_shape=shapes if len(shapes) > 1 else shapes[0],
        in_specs=specs,
        out_specs=[VMEM] * len(shapes) if len(shapes) > 1 else VMEM,
        scratch_shapes=list(scratch),
        compiler_params=pltpu.CompilerParams(vmem_limit_bytes=16 * 1024 * 1024),
        name=name,
    )


def interval_groups():
    groups = []
    for k in range(PLANES):
        early = [PLANE * ((k - 1) % PLANES) + 2 * m + 1 for m in range(GROUP)]
        groups.append(early + [PLANE * k + 2 * m for m in range(GROUP)])
    return groups


def local(timelines, knee_freq, noise_slope, noise_level, templates, interval_bounds, block_index, block_slot):
    core = lax.axis_index("c")
    group = lax.rem(lax.axis_index("z") + core, PLANES)
    segment = (PLANE * group + GROUP * (1 - core) + lax.axis_index(("y", "x"))).astype(jnp.int32).reshape(1)
    rows = timelines.reshape(OWN_DETS, SEGMENTS, SEGLEN).transpose(1, 0, 2).reshape(DETS, SEGLEN)
    scratch = [pltpu.SMEM((INTERVALS + 1,), jnp.int32)] + [pltpu.SMEM((OWN_DETS,), f32)] * 3 + [
        pltpu.VMEM((DETS, SEGLEN), f32),
        pltpu.VMEM((2, SEGMENTS, SEGMENTS), bf16),
        pltpu.VMEM((2, SEGMENTS, SEGMENTS), bf16),
        pltpu.VMEM((2, SEGMENTS, SEGMENTS), bf16),
        pltpu.VMEM((3, ROWS, SEGLEN), f32),
        pltpu.SemaphoreType.DMA((9,)),
    ]
    stored = [interval_bounds, knee_freq, noise_slope, noise_level, rows, *[jnp.asarray(t) for t in tables()]]
    line, lines = ((8, SEGLEN), f32), ((PLANE, 8, SEGLEN), f32)
    weighted, inside, outside, share = call(
        weight_kernel, [HBM] * 7, [((DETS, SEGLEN), f32), lines, lines, line], "weight", scratch
    )(*[pltpu.with_memory_space_constraint(array, pltpu.HBM) for array in stored])
    data = lax.all_to_all(
        weighted.reshape(SEGMENTS, OWN_DETS, SEGLEN), ALL, split_axis=0, concat_axis=0, tiled=True
    ).reshape(DETS, SEGLEN)
    cleaned, power = call(project_kernel, [VMEM] * 2, [((SEGLEN, DETS), f32), lines], "project")(data, templates)
    gathered = lax.all_to_all(
        power, ALL, split_axis=0, concat_axis=0, axis_index_groups=interval_groups(), tiled=True
    )
    own, message = call(halo_kernel, [VMEM] * 3, [line] * 2, "halo")(gathered, inside, outside)
    message, block_index = lax.optimization_barrier((message, block_index))
    beyond = lax.ppermute(message, "c", [(0, 1), (1, 0)])
    hot = call(slot_kernel, [SMEM] + [VMEM] * 2, [((BLOCKS, DETS), bf16)], "slots")(
        segment, block_index, block_slot.reshape(1, BLOCKS)
    )
    partial = call(bin_kernel, [VMEM] * 5, [((BLOCKS, SEGLEN), f32)], "bin")(cleaned, own, share, beyond, hot)
    spread = lax.all_to_all(
        partial.reshape(32, 8, SEGLEN), ("y", "x", "c"), split_axis=0, concat_axis=0, tiled=True
    )
    copies = call(fold_kernel, [VMEM], [((32, 8, SEGLEN), f32)], "fold")(spread)
    sums = lax.all_to_all(copies, ("z", "y"), split_axis=0, concat_axis=0, tiled=True)
    return jnp.sum(sums.reshape(8, 32, SEGLEN), axis=0)


def solution(mesh):
    whole = Mesh(mesh.devices.reshape(8, 4, 4, 2), ALL)
    return jax.shard_map(
        local,
        mesh=whole,
        in_specs=(P(ALL, None), P(ALL), P(ALL), P(ALL), P(), P(), P(), P()),
        out_specs=P(("x", "c"), None),
        check_vma=False,
    )
```

```python
import math

import jax
import jax.numpy as jnp
import numpy as np
from jax import lax
from jax.experimental import pallas as pl
from jax.experimental.pallas import tpu as pltpu
from jax.sharding import Mesh, PartitionSpec as P

DETS = 1024
SAMPLES = 32768
TEMPLATES = 512
SEGLEN = 128
SEGMENTS = 256
BLOCKS = 256
INTERVALS = 32
EPS = 1e-06
OWN_DETS = 4
HALF = SEGMENTS // 2
ROWS = HALF + 8
GROUP = 16
PLANE = 2 * GROUP
MAP_SCALE = 1.0 / math.sqrt(DETS * SAMPLES // (SEGLEN * BLOCKS))
ALL = ("z", "y", "x", "c")
PLANES = 8
bf16 = jnp.bfloat16
f32 = jnp.float32


def split_np(table):
    high = np.asarray(table, np.float32).astype(jnp.bfloat16)
    low = (table - high.astype(np.float64)).astype(np.float32).astype(jnp.bfloat16)
    return high, low


def tables():
    k = np.arange(HALF)
    c = np.arange(SEGMENTS)
    angle = 2.0 * np.pi * ((k[:, None] * c[None, :]) % SEGMENTS) / SEGMENTS
    outer = np.concatenate([np.cos(angle), -np.sin(angle)], axis=0)
    outer[HALF] = 1.0 - 2.0 * (c % 2)
    p = np.arange(SEGLEN)
    angle = 2.0 * np.pi * ((p[:, None] * p[None, :]) % SEGLEN) / SEGLEN
    inner = np.block([[np.cos(angle), -np.sin(angle)], [np.sin(angle), np.cos(angle)]])
    row = np.arange(ROWS)
    angle = 2.0 * np.pi * (row[:, None] * p[None, :]) / SAMPLES
    freq = row[:, None] + SEGMENTS * p[None, :]
    fold = np.minimum(freq, SAMPLES - freq)
    log_fold = np.where(fold > 0, np.log(np.maximum(fold, 1)), 0.0)
    return (
        np.stack([*split_np(outer), *split_np(inner), *split_np(outer.T)]),
        np.stack([np.cos(angle), np.sin(angle), log_fold]).astype(np.float32),
    )


def split(value):
    high = value.astype(bf16)
    return high, (value - high.astype(f32)).astype(bf16)


def dot3(a, b, dims):
    def one(x, y):
        return lax.dot_general(x, y, (dims, ((), ())), preferred_element_type=f32)

    rows = a[0].shape[0]
    both = one(jnp.concatenate(a, axis=0), b[0])
    return both[:rows] + (both[rows:] + one(a[0], b[1]))


NN = ((1,), (0,))
NT = ((1,), (1,))


def held_at(plane, core):
    return PLANE * ((plane + core) % PLANES) + GROUP * (1 - core)


def interval_of(bounds_ref, segment):
    at = segment * SEGLEN
    first = jnp.int32(0)
    end = jnp.int32(SAMPLES)
    for t in range(1, INTERVALS):
        bound = bounds_ref[t]
        first = jnp.where(bound <= at, jnp.maximum(first, bound), first)
        end = jnp.where(bound > at, jnp.minimum(end, bound), end)
    return first // SEGLEN, end // SEGLEN


def member_weights(bounds_ref, inside_ref, outside_ref, share_ref):
    core = lax.axis_index("c")
    base = PLANE * lax.rem(lax.axis_index("z") + core, PLANES)
    segment = base + GROUP * (1 - core) + 4 * lax.axis_index("y") + lax.axis_index("x")
    late = core == 0
    first, end = interval_of(bounds_ref, segment)
    part = 1.0 / jnp.full((8, SEGLEN), (end - first) * SEGLEN, jnp.int32).astype(f32)
    share_ref[...] = jnp.where(jnp.where(late, end > base + PLANE, first < base), part, 0.0)
    next_first, next_end = interval_of(bounds_ref, jnp.where(late, base + PLANE, base - 1))
    edge = jnp.where(late, base + PLANE == SEGMENTS, base == 0)
    next_first = jnp.where(edge, next_end, next_first)
    for member in range(PLANE):
        at = base + member
        inside_ref[member] = jnp.where((at >= first) & (at < end), part, 0.0)
        outside_ref[member] = jnp.full((8, SEGLEN), jnp.where((at >= next_first) & (at < next_end), 1.0, 0.0), f32)


def weight_kernel(
    bounds_hbm, knee_hbm, slope_hbm, level_hbm, x_hbm, tables_hbm, factors_hbm,
    out_ref, inside_ref, outside_ref, share_ref,
    bounds_ref, knee_ref, slope_ref, level_ref, x_ref, outer_ref, inner_ref, back_ref, factors_ref, sems,
):
    pairs = [
        (bounds_hbm, bounds_ref),
        (x_hbm, x_ref),
        (tables_hbm.at[pl.ds(0, 2)], outer_ref),
        (factors_hbm, factors_ref),
        (tables_hbm.at[pl.ds(2, 2)], inner_ref),
        (knee_hbm, knee_ref),
        (slope_hbm, slope_ref),
        (level_hbm, level_ref),
        (tables_hbm.at[pl.ds(4, 2)], back_ref),
    ]
    copies = [pltpu.make_async_copy(src, dst, sems.at[i]) for i, (src, dst) in enumerate(pairs)]
    for copy in copies:
        copy.start()
    copies[0].wait()
    member_weights(bounds_ref, inside_ref, outside_ref, share_ref)
    copies[1].wait()
    copies[2].wait()
    parts = [split(x_ref[pl.ds(d, SEGMENTS, stride=OWN_DETS), :]) for d in range(OWN_DETS)]
    outer = (outer_ref[0], outer_ref[1])
    samples = tuple(jnp.concatenate([part[i] for part in parts], axis=1) for i in range(2))
    section = dot3(outer, samples, NN)
    for copy in copies[3:8]:
        copy.wait()
    inner = (inner_ref[0], inner_ref[1])
    cos, sin, log_fold = factors_ref[0], factors_ref[1], factors_ref[2]
    top = lax.broadcasted_iota(jnp.int32, (8, SEGLEN), 0) == 0
    stacked = []
    for d in range(OWN_DETS):
        cut = slice(SEGLEN * d, SEGLEN * (d + 1))
        real, imag = section[:HALF, cut], section[HALF:, cut]
        real = jnp.concatenate([real, jnp.where(top, imag[:8], 0.0)], axis=0)
        imag = jnp.concatenate([jnp.where(top, 0.0, imag[:8]), imag[8:], jnp.zeros((8, SEGLEN), f32)], axis=0)
        stacked.append(jnp.concatenate([real * cos + imag * sin, imag * cos - real * sin], axis=1))
    spectrum = dot3(split(jnp.concatenate(stacked, axis=0)), inner, NN)
    row = lax.broadcasted_iota(jnp.int32, (ROWS, SEGLEN), 0)
    zero_freq = (row == 0) & (lax.broadcasted_iota(jnp.int32, (ROWS, SEGLEN), 1) == 0)
    times = jnp.where((row == 0) | (row == HALF), 1.0 / SAMPLES, 2.0 / SAMPLES).astype(f32)
    shaped = []
    for d in range(OWN_DETS):
        log_knee = jnp.log(jnp.full((1, SEGLEN), knee_ref[d], f32))
        slope = slope_ref[d]
        level = jnp.full((1, SEGLEN), level_ref[d], f32)
        ratio = jnp.exp(slope * (log_knee - log_fold))
        weight = jnp.where(zero_freq, 0.0, times / ((1.0 + ratio) * (level * level)))
        part = spectrum[ROWS * d : ROWS * (d + 1)]
        shaped.append(part * jnp.concatenate([weight, weight], axis=1))
    back = dot3(split(jnp.concatenate(shaped, axis=0)), inner, NT)
    turned = []
    for d in range(OWN_DETS):
        part = back[ROWS * d : ROWS * (d + 1)]
        real, imag = part[:, :SEGLEN], part[:, SEGLEN:]
        turn_re = real * cos - imag * sin
        turn_im = imag * cos + real * sin
        first = jnp.where(top, jnp.broadcast_to(turn_re[HALF : HALF + 1], (8, SEGLEN)), turn_im[:8])
        turned.append(jnp.concatenate([turn_re[:HALF], first, turn_im[8:HALF]], axis=0))
    copies[8].wait()
    result = dot3((back_ref[0], back_ref[1]), split(jnp.concatenate(turned, axis=1)), NN)
    for plane in range(PLANES):
        for core in range(2):
            start = held_at(plane, core)
            for d in range(OWN_DETS):
                row = (PLANE * plane + core) * OWN_DETS + d
                out_ref[pl.ds(row, GROUP, stride=2 * OWN_DETS), :] = result[
                    start : start + GROUP, SEGLEN * d : SEGLEN * (d + 1)
                ]


def project_kernel(data_ref, templates_ref, clean_ref, power_ref):
    data = data_ref[...].T
    pattern = split(templates_ref[...])
    amplitudes = dot3(split(data), pattern, NN)
    cleaned = data - dot3(split(amplitudes), pattern, NT)
    clean_ref[...] = cleaned
    power = jnp.sum(cleaned * cleaned, axis=0, keepdims=True)
    power = jnp.concatenate([power[:, SEGLEN * k : SEGLEN * (k + 1)] for k in range(8)], axis=0)
    for member in range(PLANE):
        power_ref[member] = power


def slot_kernel(segment_ref, index_ref, slot_ref, hot_ref):
    segment = segment_ref[0]
    pick = lax.broadcasted_iota(jnp.int32, (8, SEGMENTS), 1) == segment
    index = index_ref[...].astype(f32).astype(bf16)
    seen = lax.dot_general(
        jnp.where(pick, 1.0, 0.0).astype(bf16), index, (NT, ((), ())), preferred_element_type=f32
    )
    block = lax.broadcasted_iota(jnp.int32, (BLOCKS, DETS), 0)
    hot = jnp.where(jnp.broadcast_to(seen[0:1].astype(jnp.int32), (BLOCKS, DETS)) == block, 1.0, 0.0).astype(bf16)
    table = jnp.broadcast_to(slot_ref[...].astype(f32).astype(bf16), (8, BLOCKS))
    slot = lax.dot_general(table, hot, (NN, ((), ())), preferred_element_type=f32)
    row = ((block >> 4) & 7) * 32 + (block >> 7) * 16 + (block & 15)
    hot_ref[...] = jnp.where(
        jnp.broadcast_to(slot[0:1].astype(jnp.int32), (BLOCKS, DETS)) == row, 1.0, 0.0
    ).astype(bf16)


def halo_kernel(gathered_ref, weight_ref, beyond_ref, own_ref, message_ref):
    own = jnp.full((8, SEGLEN), EPS, f32)
    message = jnp.zeros((8, SEGLEN), f32)
    for member in range(PLANE):
        power = gathered_ref[member]
        own = own + weight_ref[member] * power
        message = message + beyond_ref[member] * power
    own_ref[...] = own
    message_ref[...] = message


def bin_kernel(clean_ref, own_ref, share_ref, message_ref, hot_ref, map_ref):
    inverse = 1.0 / (own_ref[...] + share_ref[...] * message_ref[...])
    values = jnp.concatenate(
        [clean_ref[:, SEGLEN * k : SEGLEN * (k + 1)] * inverse[k : k + 1] for k in range(8)], axis=1
    )
    both = lax.dot_general(
        hot_ref[...], jnp.concatenate(split(values), axis=0), (NT, ((), ())), preferred_element_type=f32
    )
    map_ref[...] = both[:, :SEGLEN] + both[:, SEGLEN:]


def fold_kernel(parts_ref, out_ref):
    total = parts_ref[0]
    for i in range(1, GROUP):
        total = total + parts_ref[i]
    out_ref[...] = total * MAP_SCALE


def copy_kernel(own_ref, other_ref, out_ref):
    total = own_ref[...] + other_ref[...]
    for i in range(GROUP):
        out_ref[i] = total


VMEM = pl.BlockSpec(memory_space=pltpu.VMEM)
SMEM = pl.BlockSpec(memory_space=pltpu.SMEM)
HBM = pl.BlockSpec(memory_space=pltpu.HBM)


def call(kernel, specs, outs, name, scratch=()):
    shapes = [pltpu.VMEM(shape, dtype) for shape, dtype in outs]
    return pl.pallas_call(
        kernel,
        out_shape=shapes if len(shapes) > 1 else shapes[0],
        in_specs=specs,
        out_specs=[VMEM] * len(shapes) if len(shapes) > 1 else VMEM,
        scratch_shapes=list(scratch),
        compiler_params=pltpu.CompilerParams(vmem_limit_bytes=16 * 1024 * 1024),
        name=name,
    )


def interval_groups():
    groups = []
    for k in range(PLANES):
        early = [PLANE * ((k - 1) % PLANES) + 2 * m + 1 for m in range(GROUP)]
        groups.append(early + [PLANE * k + 2 * m for m in range(GROUP)])
    return groups


def half_groups(before, after):
    groups = []
    for outer in range(2):
        order = [3 * outer, 3 * outer + 1 - 2 * outer]
        groups.append(
            [(b * 4 + y) * len(after) + a for b in before for y in order for a in after]
        )
    return groups


def local(timelines, knee_freq, noise_slope, noise_level, templates, interval_bounds, block_index, block_slot):
    core = lax.axis_index("c")
    group = lax.rem(lax.axis_index("z") + core, PLANES)
    segment = (PLANE * group + GROUP * (1 - core) + lax.axis_index(("y", "x"))).astype(jnp.int32).reshape(1)
    rows = timelines.reshape(OWN_DETS, SEGMENTS, SEGLEN).transpose(1, 0, 2).reshape(DETS, SEGLEN)
    scratch = [pltpu.SMEM((INTERVALS + 1,), jnp.int32)] + [pltpu.SMEM((OWN_DETS,), f32)] * 3 + [
        pltpu.VMEM((DETS, SEGLEN), f32),
        pltpu.VMEM((2, SEGMENTS, SEGMENTS), bf16),
        pltpu.VMEM((2, SEGMENTS, SEGMENTS), bf16),
        pltpu.VMEM((2, SEGMENTS, SEGMENTS), bf16),
        pltpu.VMEM((3, ROWS, SEGLEN), f32),
        pltpu.SemaphoreType.DMA((9,)),
    ]
    stored = [interval_bounds, knee_freq, noise_slope, noise_level, rows, *[jnp.asarray(t) for t in tables()]]
    line, lines = ((8, SEGLEN), f32), ((PLANE, 8, SEGLEN), f32)
    weighted, inside, outside, share = call(
        weight_kernel, [HBM] * 7, [((DETS, SEGLEN), f32), lines, lines, line], "weight", scratch
    )(*[pltpu.with_memory_space_constraint(array, pltpu.HBM) for array in stored])
    data = lax.all_to_all(
        weighted.reshape(SEGMENTS, OWN_DETS, SEGLEN), ALL, split_axis=0, concat_axis=0, tiled=True
    ).reshape(DETS, SEGLEN)
    cleaned, power = call(project_kernel, [VMEM] * 2, [((SEGLEN, DETS), f32), lines], "project")(data, templates)
    gathered = lax.all_to_all(
        power, ALL, split_axis=0, concat_axis=0, axis_index_groups=interval_groups(), tiled=True
    )
    own, message = call(halo_kernel, [VMEM] * 3, [line] * 2, "halo")(gathered, inside, outside)
    message, block_index = lax.optimization_barrier((message, block_index))
    beyond = lax.ppermute(message, "c", [(0, 1), (1, 0)])
    hot = call(slot_kernel, [SMEM] + [VMEM] * 2, [((BLOCKS, DETS), bf16)], "slots")(
        segment, block_index, block_slot.reshape(1, BLOCKS)
    )
    partial = call(bin_kernel, [VMEM] * 5, [((BLOCKS, SEGLEN), f32)], "bin")(cleaned, own, share, beyond, hot)
    spread = lax.all_to_all(
        partial.reshape(GROUP, GROUP, SEGLEN), ("y", "x", "c"), split_axis=0, concat_axis=0,
        axis_index_groups=half_groups(range(1), range(8)), tiled=True,
    )
    half = call(fold_kernel, [VMEM], [((GROUP, SEGLEN), f32)], "fold")(spread)
    mirror = lax.ppermute(half, "y", [(i, 3 - i) for i in range(4)])
    copies = call(copy_kernel, [VMEM] * 2, [((GROUP, GROUP, SEGLEN), f32)], "copies")(half, mirror)
    sums = lax.all_to_all(
        copies, ("z", "y"), split_axis=0, concat_axis=0,
        axis_index_groups=half_groups(range(PLANES), range(1)), tiled=True,
    )
    return jnp.sum(sums.reshape(8, 32, SEGLEN), axis=0)


def solution(mesh):
    whole = Mesh(mesh.devices.reshape(8, 4, 4, 2), ALL)
    return jax.shard_map(
        local,
        mesh=whole,
        in_specs=(P(ALL, None), P(ALL), P(ALL), P(ALL), P(), P(), P(), P()),
        out_specs=P(("x", "c"), None),
        check_vma=False,
    )
```

```python
import math

import jax
import jax.numpy as jnp
import numpy as np
from jax import lax
from jax.experimental import pallas as pl
from jax.experimental.pallas import tpu as pltpu
from jax.sharding import Mesh, PartitionSpec as P

DETS = 1024
SAMPLES = 32768
TEMPLATES = 512
SEGLEN = 128
SEGMENTS = 256
BLOCKS = 256
INTERVALS = 32
EPS = 1e-06
OWN_DETS = 4
HALF = SEGMENTS // 2
ROWS = HALF + 8
GROUP = 16
PLANE = 2 * GROUP
MAP_SCALE = 1.0 / math.sqrt(DETS * SAMPLES // (SEGLEN * BLOCKS))
ALL = ("z", "y", "x", "c")
PLANES = 8
bf16 = jnp.bfloat16
f32 = jnp.float32


def split_np(table):
    high = np.asarray(table, np.float32).astype(jnp.bfloat16)
    low = (table - high.astype(np.float64)).astype(np.float32).astype(jnp.bfloat16)
    return high, low


def tables():
    k = np.arange(HALF)
    c = np.arange(SEGMENTS)
    angle = 2.0 * np.pi * ((k[:, None] * c[None, :]) % SEGMENTS) / SEGMENTS
    outer = np.concatenate([np.cos(angle), -np.sin(angle)], axis=0)
    outer[HALF] = 1.0 - 2.0 * (c % 2)
    p = np.arange(SEGLEN)
    angle = 2.0 * np.pi * ((p[:, None] * p[None, :]) % SEGLEN) / SEGLEN
    inner = np.block([[np.cos(angle), -np.sin(angle)], [np.sin(angle), np.cos(angle)]])
    row = np.arange(ROWS)
    angle = 2.0 * np.pi * (row[:, None] * p[None, :]) / SAMPLES
    freq = row[:, None] + SEGMENTS * p[None, :]
    fold = np.minimum(freq, SAMPLES - freq)
    log_fold = np.where(fold > 0, np.log(np.maximum(fold, 1)), 0.0)
    return (
        np.stack([*split_np(outer), *split_np(inner), *split_np(outer.T)]),
        np.stack([np.cos(angle), np.sin(angle), log_fold]).astype(np.float32),
    )


def split(value):
    high = value.astype(bf16)
    return high, (value - high.astype(f32)).astype(bf16)


def dot3(a, b, dims):
    def one(x, y):
        return lax.dot_general(x, y, (dims, ((), ())), preferred_element_type=f32)

    rows = a[0].shape[0]
    both = one(jnp.concatenate(a, axis=0), b[0])
    return both[:rows] + (both[rows:] + one(a[0], b[1]))


NN = ((1,), (0,))
NT = ((1,), (1,))


def held_at(plane, half):
    return PLANE * plane + GROUP * (half ^ (plane & 1))


def interval_of(bounds_ref, segment):
    at = segment * SEGLEN
    first = jnp.int32(0)
    end = jnp.int32(SAMPLES)
    for t in range(1, INTERVALS):
        bound = bounds_ref[t]
        first = jnp.where(bound <= at, jnp.maximum(first, bound), first)
        end = jnp.where(bound > at, jnp.minimum(end, bound), end)
    return first // SEGLEN, end // SEGLEN


def member_weights(bounds_ref, inside_ref, near_ref, far_ref, share_ref):
    z, y = lax.axis_index("z"), lax.axis_index("y")
    odd = (y >> 1) ^ (z & 1)
    base = PLANE * z + GROUP * odd
    segment = base + 8 * (y & 1) + 2 * lax.axis_index("x") + lax.axis_index("c")
    first, end = interval_of(bounds_ref, segment)
    part = 1.0 / jnp.full((8, SEGLEN), (end - first) * SEGLEN, jnp.int32).astype(f32)
    for member in range(GROUP):
        at = base + member
        inside_ref[member] = jnp.where((at >= first) & (at < end), part, 0.0)
    for i, message_ref in ((0, near_ref), (1, far_ref)):
        ahead = odd == i
        share_ref[i] = jnp.where(jnp.where(ahead, end > base + GROUP, first < base), part, 0.0)
        next_first, next_end = interval_of(bounds_ref, jnp.where(ahead, base + GROUP, base - 1))
        edge = jnp.where(ahead, base + GROUP == SEGMENTS, base == 0)
        next_first = jnp.where(edge, next_end, next_first)
        for member in range(GROUP):
            at = base + member
            inside = (at >= next_first) & (at < next_end)
            message_ref[member] = jnp.full((8, SEGLEN), jnp.where(inside, 1.0, 0.0), f32)


def weight_kernel(
    bounds_hbm, knee_hbm, slope_hbm, level_hbm, x_hbm, tables_hbm, factors_hbm,
    out_ref, inside_ref, near_ref, far_ref, share_ref,
    bounds_ref, knee_ref, slope_ref, level_ref, x_ref, outer_ref, inner_ref, back_ref, factors_ref, sems,
):
    pairs = [
        (bounds_hbm, bounds_ref),
        (x_hbm, x_ref),
        (tables_hbm.at[pl.ds(0, 2)], outer_ref),
        (factors_hbm, factors_ref),
        (tables_hbm.at[pl.ds(2, 2)], inner_ref),
        (knee_hbm, knee_ref),
        (slope_hbm, slope_ref),
        (level_hbm, level_ref),
        (tables_hbm.at[pl.ds(4, 2)], back_ref),
    ]
    copies = [pltpu.make_async_copy(src, dst, sems.at[i]) for i, (src, dst) in enumerate(pairs)]
    for copy in copies:
        copy.start()
    copies[0].wait()
    member_weights(bounds_ref, inside_ref, near_ref, far_ref, share_ref)
    copies[1].wait()
    copies[2].wait()
    parts = [split(x_ref[pl.ds(d, SEGMENTS, stride=OWN_DETS), :]) for d in range(OWN_DETS)]
    outer = (outer_ref[0], outer_ref[1])
    samples = tuple(jnp.concatenate([part[i] for part in parts], axis=1) for i in range(2))
    section = dot3(outer, samples, NN)
    for copy in copies[3:8]:
        copy.wait()
    inner = (inner_ref[0], inner_ref[1])
    cos, sin, log_fold = factors_ref[0], factors_ref[1], factors_ref[2]
    top = lax.broadcasted_iota(jnp.int32, (8, SEGLEN), 0) == 0
    stacked = []
    for d in range(OWN_DETS):
        cut = slice(SEGLEN * d, SEGLEN * (d + 1))
        real, imag = section[:HALF, cut], section[HALF:, cut]
        real = jnp.concatenate([real, jnp.where(top, imag[:8], 0.0)], axis=0)
        imag = jnp.concatenate([jnp.where(top, 0.0, imag[:8]), imag[8:], jnp.zeros((8, SEGLEN), f32)], axis=0)
        stacked.append(jnp.concatenate([real * cos + imag * sin, imag * cos - real * sin], axis=1))
    spectrum = dot3(split(jnp.concatenate(stacked, axis=0)), inner, NN)
    row = lax.broadcasted_iota(jnp.int32, (ROWS, SEGLEN), 0)
    zero_freq = (row == 0) & (lax.broadcasted_iota(jnp.int32, (ROWS, SEGLEN), 1) == 0)
    times = jnp.where((row == 0) | (row == HALF), 1.0 / SAMPLES, 2.0 / SAMPLES).astype(f32)
    shaped = []
    for d in range(OWN_DETS):
        log_knee = jnp.log(jnp.full((1, SEGLEN), knee_ref[d], f32))
        slope = slope_ref[d]
        level = jnp.full((1, SEGLEN), level_ref[d], f32)
        ratio = jnp.exp(slope * (log_knee - log_fold))
        weight = jnp.where(zero_freq, 0.0, times / ((1.0 + ratio) * (level * level)))
        part = spectrum[ROWS * d : ROWS * (d + 1)]
        shaped.append(part * jnp.concatenate([weight, weight], axis=1))
    back = dot3(split(jnp.concatenate(shaped, axis=0)), inner, NT)
    turned = []
    for d in range(OWN_DETS):
        part = back[ROWS * d : ROWS * (d + 1)]
        real, imag = part[:, :SEGLEN], part[:, SEGLEN:]
        turn_re = real * cos - imag * sin
        turn_im = imag * cos + real * sin
        first = jnp.where(top, jnp.broadcast_to(turn_re[HALF : HALF + 1], (8, SEGLEN)), turn_im[:8])
        turned.append(jnp.concatenate([turn_re[:HALF], first, turn_im[8:HALF]], axis=0))
    copies[8].wait()
    result = dot3((back_ref[0], back_ref[1]), split(jnp.concatenate(turned, axis=1)), NN)
    for plane in range(PLANES):
        for side in range(2):
            start = held_at(plane, side)
            for d in range(OWN_DETS):
                row = (PLANE * plane + GROUP * side) * OWN_DETS + d
                out_ref[pl.ds(row, GROUP, stride=OWN_DETS), :] = result[
                    start : start + GROUP, SEGLEN * d : SEGLEN * (d + 1)
                ]


def project_kernel(data_ref, templates_ref, clean_ref, power_ref):
    data = data_ref[...].T
    pattern = split(templates_ref[...])
    amplitudes = dot3(split(data), pattern, NN)
    cleaned = data - dot3(split(amplitudes), pattern, NT)
    clean_ref[...] = cleaned
    power = jnp.sum(cleaned * cleaned, axis=0, keepdims=True)
    power = jnp.concatenate([power[:, SEGLEN * k : SEGLEN * (k + 1)] for k in range(8)], axis=0)
    for member in range(GROUP):
        power_ref[member] = power


def slot_kernel(segment_ref, index_ref, slot_ref, hot_ref):
    segment = segment_ref[0]
    pick = lax.broadcasted_iota(jnp.int32, (8, SEGMENTS), 1) == segment
    index = index_ref[...].astype(f32).astype(bf16)
    seen = lax.dot_general(
        jnp.where(pick, 1.0, 0.0).astype(bf16), index, (NT, ((), ())), preferred_element_type=f32
    )
    block = lax.broadcasted_iota(jnp.int32, (BLOCKS, DETS), 0)
    hot = jnp.where(jnp.broadcast_to(seen[0:1].astype(jnp.int32), (BLOCKS, DETS)) == block, 1.0, 0.0).astype(bf16)
    table = jnp.broadcast_to(slot_ref[...].astype(f32).astype(bf16), (8, BLOCKS))
    slot = lax.dot_general(table, hot, (NN, ((), ())), preferred_element_type=f32)
    row = ((block >> 3) & 7) * 32 + (block >> 6) * 8 + (block & 7)
    hot_ref[...] = jnp.where(
        jnp.broadcast_to(slot[0:1].astype(jnp.int32), (BLOCKS, DETS)) == row, 1.0, 0.0
    ).astype(bf16)


def halo_kernel(gathered_ref, inside_ref, near_ref, far_ref, own_ref, near_out, far_out):
    own = jnp.full((8, SEGLEN), EPS, f32)
    near = jnp.zeros((8, SEGLEN), f32)
    far = near
    for member in range(GROUP):
        power = gathered_ref[member]
        own = own + inside_ref[member] * power
        near = near + near_ref[member] * power
        far = far + far_ref[member] * power
    own_ref[...] = own
    near_out[...] = near
    far_out[...] = far


def bin_kernel(clean_ref, own_ref, share_ref, near_ref, far_ref, hot_ref, map_ref):
    inverse = 1.0 / (own_ref[...] + share_ref[0] * near_ref[...] + share_ref[1] * far_ref[...])
    values = jnp.concatenate(
        [clean_ref[:, SEGLEN * k : SEGLEN * (k + 1)] * inverse[k : k + 1] for k in range(8)], axis=1
    )
    both = lax.dot_general(
        hot_ref[...], jnp.concatenate(split(values), axis=0), (NT, ((), ())), preferred_element_type=f32
    )
    map_ref[...] = both[:, :SEGLEN] + both[:, SEGLEN:]


def fold_kernel(parts_ref, out_ref):
    total = parts_ref[0]
    for i in range(1, parts_ref.shape[0]):
        total = total + parts_ref[i]
    total = total * MAP_SCALE
    for i in range(out_ref.shape[0]):
        out_ref[i] = total


VMEM = pl.BlockSpec(memory_space=pltpu.VMEM)
SMEM = pl.BlockSpec(memory_space=pltpu.SMEM)
HBM = pl.BlockSpec(memory_space=pltpu.HBM)


def call(kernel, specs, outs, name, scratch=()):
    shapes = [pltpu.VMEM(shape, dtype) for shape, dtype in outs]
    return pl.pallas_call(
        kernel,
        out_shape=shapes if len(shapes) > 1 else shapes[0],
        in_specs=specs,
        out_specs=[VMEM] * len(shapes) if len(shapes) > 1 else VMEM,
        scratch_shapes=list(scratch),
        compiler_params=pltpu.CompilerParams(vmem_limit_bytes=16 * 1024 * 1024),
        name=name,
    )


def far_pairs():
    pairs = []
    for z in range(PLANES):
        for y in range(4):
            z_to = z ^ 1 if y >> 1 else (z + (1 if z % 2 else -1)) % PLANES
            pairs.append((4 * z + y, 4 * z_to + y))
    return pairs


def local(timelines, knee_freq, noise_slope, noise_level, templates, interval_bounds, block_index, block_slot):
    z, y = lax.axis_index("z"), lax.axis_index("y")
    base = PLANE * z + GROUP * ((y >> 1) ^ (z & 1))
    segment = (base + 8 * (y & 1) + lax.axis_index(("x", "c"))).astype(jnp.int32).reshape(1)
    rows = timelines.reshape(OWN_DETS, SEGMENTS, SEGLEN).transpose(1, 0, 2).reshape(DETS, SEGLEN)
    scratch = [pltpu.SMEM((INTERVALS + 1,), jnp.int32)] + [pltpu.SMEM((OWN_DETS,), f32)] * 3 + [
        pltpu.VMEM((DETS, SEGLEN), f32),
        pltpu.VMEM((2, SEGMENTS, SEGMENTS), bf16),
        pltpu.VMEM((2, SEGMENTS, SEGMENTS), bf16),
        pltpu.VMEM((2, SEGMENTS, SEGMENTS), bf16),
        pltpu.VMEM((3, ROWS, SEGLEN), f32),
        pltpu.SemaphoreType.DMA((9,)),
    ]
    stored = [interval_bounds, knee_freq, noise_slope, noise_level, rows, *[jnp.asarray(t) for t in tables()]]
    line, lines, two = [((*lead, 8, SEGLEN), f32) for lead in ((), (GROUP,), (2,))]
    weighted, inside, to_near, to_far, share = call(
        weight_kernel, [HBM] * 7, [((DETS, SEGLEN), f32), lines, lines, lines, two], "weight", scratch
    )(*[pltpu.with_memory_space_constraint(array, pltpu.HBM) for array in stored])
    data = lax.all_to_all(
        weighted.reshape(SEGMENTS, OWN_DETS, SEGLEN), ALL, split_axis=0, concat_axis=0, tiled=True
    ).reshape(DETS, SEGLEN)
    cleaned, power = call(project_kernel, [VMEM] * 2, [((SEGLEN, DETS), f32), lines], "project")(data, templates)
    gathered = lax.all_to_all(
        power, ("y", "x", "c"), split_axis=0, concat_axis=0,
        axis_index_groups=[list(range(16)), list(range(16, 32))], tiled=True,
    )
    own, near, far = call(halo_kernel, [VMEM] * 4, [line] * 3, "halo")(gathered, inside, to_near, to_far)
    near, far, block_index = lax.optimization_barrier((near, far, block_index))
    near = lax.ppermute(near, "y", [(i, 3 - i) for i in range(4)])
    far = lax.ppermute(far, ("z", "y"), far_pairs())
    hot = call(slot_kernel, [SMEM] + [VMEM] * 2, [((BLOCKS, DETS), bf16)], "slots")(
        segment, block_index, block_slot.reshape(1, BLOCKS)
    )
    partial = call(bin_kernel, [VMEM] * 6, [((BLOCKS, SEGLEN), f32)], "bin")(
        cleaned, own, share, near, far, hot
    )
    spread = lax.all_to_all(
        partial.reshape(32, 8, SEGLEN), ("y", "x", "c"), split_axis=0, concat_axis=0, tiled=True
    )
    copies = call(fold_kernel, [VMEM], [((32, 8, SEGLEN), f32)], "fold")(spread)
    sums = lax.all_to_all(copies, ("z", "y"), split_axis=0, concat_axis=0, tiled=True)
    return jnp.sum(sums.reshape(8, 32, SEGLEN), axis=0)


def solution(mesh):
    whole = Mesh(mesh.devices.reshape(8, 4, 4, 2), ALL)
    return jax.shard_map(
        local,
        mesh=whole,
        in_specs=(P(ALL, None), P(ALL), P(ALL), P(ALL), P(), P(), P(), P()),
        out_specs=P(("x", "c"), None),
        check_vma=False,
    )
```

```python
import math

import jax
import jax.numpy as jnp
import numpy as np
from jax import lax
from jax.experimental import pallas as pl
from jax.experimental.pallas import tpu as pltpu
from jax.sharding import Mesh, PartitionSpec as P

DETS = 1024
SAMPLES = 32768
TEMPLATES = 512
SEGLEN = 128
SEGMENTS = 256
BLOCKS = 256
INTERVALS = 32
EPS = 1e-06
OWN_DETS = 4
HALF = SEGMENTS // 2
ROWS = HALF + 8
GROUP = 16
PLANE = 2 * GROUP
MAP_SCALE = 1.0 / math.sqrt(DETS * SAMPLES // (SEGLEN * BLOCKS))
ALL = ("z", "y", "x", "c")
PLANES = 8
bf16 = jnp.bfloat16
f32 = jnp.float32


def split_np(table):
    high = np.asarray(table, np.float32).astype(jnp.bfloat16)
    low = (table - high.astype(np.float64)).astype(np.float32).astype(jnp.bfloat16)
    return high, low


def tables():
    k = np.arange(HALF)
    c = np.arange(SEGMENTS)
    angle = 2.0 * np.pi * ((k[:, None] * c[None, :]) % SEGMENTS) / SEGMENTS
    outer = np.concatenate([np.cos(angle), -np.sin(angle)], axis=0)
    outer[HALF] = 1.0 - 2.0 * (c % 2)
    p = np.arange(SEGLEN)
    angle = 2.0 * np.pi * ((p[:, None] * p[None, :]) % SEGLEN) / SEGLEN
    inner = np.block([[np.cos(angle), -np.sin(angle)], [np.sin(angle), np.cos(angle)]])
    row = np.arange(ROWS)
    angle = 2.0 * np.pi * (row[:, None] * p[None, :]) / SAMPLES
    freq = row[:, None] + SEGMENTS * p[None, :]
    fold = np.minimum(freq, SAMPLES - freq)
    log_fold = np.where(fold > 0, np.log(np.maximum(fold, 1)), 0.0)
    return (
        np.stack([*split_np(outer), *split_np(inner), *split_np(outer.T)]),
        np.stack([np.cos(angle), np.sin(angle), log_fold]).astype(np.float32),
    )


def split(value):
    high = value.astype(bf16)
    return high, (value - high.astype(f32)).astype(bf16)


def dot3(a, b, dims):
    def one(x, y):
        return lax.dot_general(x, y, (dims, ((), ())), preferred_element_type=f32)

    rows = a[0].shape[0]
    both = one(jnp.concatenate(a, axis=0), b[0])
    return both[:rows] + (both[rows:] + one(a[0], b[1]))


NN = ((1,), (0,))
NT = ((1,), (1,))


def held_at(plane, half):
    return PLANE * plane + GROUP * (half ^ (plane & 1))


def interval_of(bounds_ref, segment):
    at = segment * SEGLEN
    first = jnp.int32(0)
    end = jnp.int32(SAMPLES)
    for t in range(1, INTERVALS):
        bound = bounds_ref[t]
        first = jnp.where(bound <= at, jnp.maximum(first, bound), first)
        end = jnp.where(bound > at, jnp.minimum(end, bound), end)
    return first // SEGLEN, end // SEGLEN


def member_weights(bounds_ref, inside_ref, near_ref, far_ref, share_ref):
    z, y = lax.axis_index("z"), lax.axis_index("y")
    odd = (y >> 1) ^ (z & 1)
    base = PLANE * z + GROUP * odd
    segment = base + 8 * (y & 1) + 2 * lax.axis_index("x") + lax.axis_index("c")
    first, end = interval_of(bounds_ref, segment)
    part = 1.0 / jnp.full((8, SEGLEN), (end - first) * SEGLEN, jnp.int32).astype(f32)
    for member in range(GROUP):
        at = base + member
        inside_ref[member] = jnp.where((at >= first) & (at < end), part, 0.0)
    for i, message_ref in ((0, near_ref), (1, far_ref)):
        ahead = odd == i
        share_ref[i] = jnp.where(jnp.where(ahead, end > base + GROUP, first < base), part, 0.0)
        next_first, next_end = interval_of(bounds_ref, jnp.where(ahead, base + GROUP, base - 1))
        edge = jnp.where(ahead, base + GROUP == SEGMENTS, base == 0)
        next_first = jnp.where(edge, next_end, next_first)
        for member in range(GROUP):
            at = base + member
            inside = (at >= next_first) & (at < next_end)
            message_ref[member] = jnp.full((8, SEGLEN), jnp.where(inside, 1.0, 0.0), f32)


def weight_kernel(
    bounds_hbm, knee_hbm, slope_hbm, level_hbm, x_hbm, tables_hbm, factors_hbm,
    out_ref, inside_ref, near_ref, far_ref, share_ref,
    bounds_ref, knee_ref, slope_ref, level_ref, x_ref, outer_ref, inner_ref, back_ref, factors_ref, sems,
):
    pairs = [
        (bounds_hbm, bounds_ref),
        (x_hbm, x_ref),
        (tables_hbm.at[pl.ds(0, 2)], outer_ref),
        (factors_hbm, factors_ref),
        (tables_hbm.at[pl.ds(2, 2)], inner_ref),
        (knee_hbm, knee_ref),
        (slope_hbm, slope_ref),
        (level_hbm, level_ref),
        (tables_hbm.at[pl.ds(4, 2)], back_ref),
    ]
    copies = [pltpu.make_async_copy(src, dst, sems.at[i]) for i, (src, dst) in enumerate(pairs)]
    for copy in copies:
        copy.start()
    copies[0].wait()
    member_weights(bounds_ref, inside_ref, near_ref, far_ref, share_ref)
    copies[1].wait()
    copies[2].wait()
    parts = [split(x_ref[pl.ds(d, SEGMENTS, stride=OWN_DETS), :]) for d in range(OWN_DETS)]
    outer = (outer_ref[0], outer_ref[1])
    samples = tuple(jnp.concatenate([part[i] for part in parts], axis=1) for i in range(2))
    section = dot3(outer, samples, NN)
    for copy in copies[3:8]:
        copy.wait()
    inner = (inner_ref[0], inner_ref[1])
    cos, sin, log_fold = factors_ref[0], factors_ref[1], factors_ref[2]
    top = lax.broadcasted_iota(jnp.int32, (8, SEGLEN), 0) == 0
    stacked = []
    for d in range(OWN_DETS):
        cut = slice(SEGLEN * d, SEGLEN * (d + 1))
        real, imag = section[:HALF, cut], section[HALF:, cut]
        real = jnp.concatenate([real, jnp.where(top, imag[:8], 0.0)], axis=0)
        imag = jnp.concatenate([jnp.where(top, 0.0, imag[:8]), imag[8:], jnp.zeros((8, SEGLEN), f32)], axis=0)
        stacked.append(jnp.concatenate([real * cos + imag * sin, imag * cos - real * sin], axis=1))
    spectrum = dot3(split(jnp.concatenate(stacked, axis=0)), inner, NN)
    row = lax.broadcasted_iota(jnp.int32, (ROWS, SEGLEN), 0)
    zero_freq = (row == 0) & (lax.broadcasted_iota(jnp.int32, (ROWS, SEGLEN), 1) == 0)
    times = jnp.where((row == 0) | (row == HALF), 1.0 / SAMPLES, 2.0 / SAMPLES).astype(f32)
    shaped = []
    for d in range(OWN_DETS):
        log_knee = jnp.log(jnp.full((1, SEGLEN), knee_ref[d], f32))
        slope = slope_ref[d]
        level = jnp.full((1, SEGLEN), level_ref[d], f32)
        ratio = jnp.exp(slope * (log_knee - log_fold))
        weight = jnp.where(zero_freq, 0.0, times / ((1.0 + ratio) * (level * level)))
        part = spectrum[ROWS * d : ROWS * (d + 1)]
        shaped.append(part * jnp.concatenate([weight, weight], axis=1))
    back = dot3(split(jnp.concatenate(shaped, axis=0)), inner, NT)
    turned = []
    for d in range(OWN_DETS):
        part = back[ROWS * d : ROWS * (d + 1)]
        real, imag = part[:, :SEGLEN], part[:, SEGLEN:]
        turn_re = real * cos - imag * sin
        turn_im = imag * cos + real * sin
        first = jnp.where(top, jnp.broadcast_to(turn_re[HALF : HALF + 1], (8, SEGLEN)), turn_im[:8])
        turned.append(jnp.concatenate([turn_re[:HALF], first, turn_im[8:HALF]], axis=0))
    copies[8].wait()
    result = dot3((back_ref[0], back_ref[1]), split(jnp.concatenate(turned, axis=1)), NN)
    for plane in range(PLANES):
        for side in range(2):
            start = held_at(plane, side)
            for d in range(OWN_DETS):
                row = (PLANE * plane + GROUP * side) * OWN_DETS + d
                out_ref[pl.ds(row, GROUP, stride=OWN_DETS), :] = result[
                    start : start + GROUP, SEGLEN * d : SEGLEN * (d + 1)
                ]


def project_kernel(data_ref, templates_ref, clean_ref, power_ref):
    data = data_ref[...].T
    pattern = split(templates_ref[...])
    amplitudes = dot3(split(data), pattern, NN)
    cleaned = data - dot3(split(amplitudes), pattern, NT)
    clean_ref[...] = cleaned
    power = jnp.sum(cleaned * cleaned, axis=0, keepdims=True)
    power = jnp.concatenate([power[:, SEGLEN * k : SEGLEN * (k + 1)] for k in range(8)], axis=0)
    for member in range(GROUP):
        power_ref[member] = power


def slot_kernel(segment_ref, index_ref, slot_ref, hot_ref):
    segment = segment_ref[0]
    pick = lax.broadcasted_iota(jnp.int32, (8, SEGMENTS), 1) == segment
    index = index_ref[...].astype(f32).astype(bf16)
    seen = lax.dot_general(
        jnp.where(pick, 1.0, 0.0).astype(bf16), index, (NT, ((), ())), preferred_element_type=f32
    )
    block = lax.broadcasted_iota(jnp.int32, (BLOCKS, DETS), 0)
    hot = jnp.where(jnp.broadcast_to(seen[0:1].astype(jnp.int32), (BLOCKS, DETS)) == block, 1.0, 0.0).astype(bf16)
    table = jnp.broadcast_to(slot_ref[...].astype(f32).astype(bf16), (8, BLOCKS))
    slot = lax.dot_general(table, hot, (NN, ((), ())), preferred_element_type=f32)
    row = ((block >> 3) & 7) * 32 + (block >> 6) * 8 + (block & 7)
    hot_ref[...] = jnp.where(
        jnp.broadcast_to(slot[0:1].astype(jnp.int32), (BLOCKS, DETS)) == row, 1.0, 0.0
    ).astype(bf16)


def halo_kernel(gathered_ref, inside_ref, near_ref, far_ref, own_ref, near_out, far_out):
    own = jnp.full((8, SEGLEN), EPS, f32)
    near = jnp.zeros((8, SEGLEN), f32)
    far = near
    for member in range(GROUP):
        power = gathered_ref[member]
        own = own + inside_ref[member] * power
        near = near + near_ref[member] * power
        far = far + far_ref[member] * power
    own_ref[...] = own
    near_out[...] = near
    far_out[...] = far


def bin_kernel(clean_ref, own_ref, share_ref, near_ref, far_ref, hot_ref, map_ref):
    inverse = 1.0 / (own_ref[...] + share_ref[0] * near_ref[...] + share_ref[1] * far_ref[...])
    values = jnp.concatenate(
        [clean_ref[:, SEGLEN * k : SEGLEN * (k + 1)] * inverse[k : k + 1] for k in range(8)], axis=1
    )
    both = lax.dot_general(
        hot_ref[...], jnp.concatenate(split(values), axis=0), (NT, ((), ())), preferred_element_type=f32
    )
    map_ref[...] = both[:, :SEGLEN] + both[:, SEGLEN:]


def fold_kernel(parts_ref, out_ref):
    total = parts_ref[0]
    for i in range(1, parts_ref.shape[0]):
        total = total + parts_ref[i]
    total = total * MAP_SCALE
    for i in range(out_ref.shape[0]):
        out_ref[i] = total


VMEM = pl.BlockSpec(memory_space=pltpu.VMEM)
SMEM = pl.BlockSpec(memory_space=pltpu.SMEM)
HBM = pl.BlockSpec(memory_space=pltpu.HBM)


def call(kernel, specs, outs, name, scratch=()):
    shapes = [pltpu.VMEM(shape, dtype) for shape, dtype in outs]
    return pl.pallas_call(
        kernel,
        out_shape=shapes if len(shapes) > 1 else shapes[0],
        in_specs=specs,
        out_specs=[VMEM] * len(shapes) if len(shapes) > 1 else VMEM,
        scratch_shapes=list(scratch),
        compiler_params=pltpu.CompilerParams(vmem_limit_bytes=16 * 1024 * 1024),
        name=name,
    )


def far_pairs():
    pairs = []
    for z in range(PLANES):
        for y in range(4):
            z_to = z ^ 1 if y >> 1 else (z + (1 if z % 2 else -1)) % PLANES
            pairs.append((4 * z + y, 4 * z_to + y))
    return pairs


def local(timelines, knee_freq, noise_slope, noise_level, templates, interval_bounds, block_index, block_slot):
    z, y = lax.axis_index("z"), lax.axis_index("y")
    base = PLANE * z + GROUP * ((y >> 1) ^ (z & 1))
    segment = (base + 8 * (y & 1) + lax.axis_index(("x", "c"))).astype(jnp.int32).reshape(1)
    rows = timelines.reshape(OWN_DETS, SEGMENTS, SEGLEN).transpose(1, 0, 2).reshape(DETS, SEGLEN)
    scratch = [pltpu.SMEM((INTERVALS + 1,), jnp.int32)] + [pltpu.SMEM((OWN_DETS,), f32)] * 3 + [
        pltpu.VMEM((DETS, SEGLEN), f32),
        pltpu.VMEM((2, SEGMENTS, SEGMENTS), bf16),
        pltpu.VMEM((2, SEGMENTS, SEGMENTS), bf16),
        pltpu.VMEM((2, SEGMENTS, SEGMENTS), bf16),
        pltpu.VMEM((3, ROWS, SEGLEN), f32),
        pltpu.SemaphoreType.DMA((9,)),
    ]
    stored = [interval_bounds, knee_freq, noise_slope, noise_level, rows, *[jnp.asarray(t) for t in tables()]]
    line, lines, two = [((*lead, 8, SEGLEN), f32) for lead in ((), (GROUP,), (2,))]
    weighted, inside, to_near, to_far, share = call(
        weight_kernel, [HBM] * 7, [((DETS, SEGLEN), f32), lines, lines, lines, two], "weight", scratch
    )(*[pltpu.with_memory_space_constraint(array, pltpu.HBM) for array in stored])
    data = lax.all_to_all(
        weighted.reshape(SEGMENTS, OWN_DETS, SEGLEN), ALL, split_axis=0, concat_axis=0, tiled=True
    ).reshape(DETS, SEGLEN)
    cleaned, power = call(project_kernel, [VMEM] * 2, [((SEGLEN, DETS), f32), lines], "project")(data, templates)
    gathered = lax.all_to_all(
        power, ("y", "x", "c"), split_axis=0, concat_axis=0,
        axis_index_groups=[list(range(16)), list(range(16, 32))], tiled=True,
    )
    own, near, far = call(halo_kernel, [VMEM] * 4, [line] * 3, "halo")(gathered, inside, to_near, to_far)
    near, far, block_index = lax.optimization_barrier((near, far, block_index))
    near = lax.ppermute(near, "y", [(i, 3 - i) for i in range(4)])
    far = lax.ppermute(far, ("z", "y"), far_pairs())
    hot = call(slot_kernel, [SMEM] + [VMEM] * 2, [((BLOCKS, DETS), bf16)], "slots")(
        segment, block_index, block_slot.reshape(1, BLOCKS)
    )
    partial = call(bin_kernel, [VMEM] * 6, [((BLOCKS, SEGLEN), f32)], "bin")(
        cleaned, own, share, near, far, hot
    )
    spread = lax.all_to_all(
        partial.reshape(32, 8, SEGLEN), ("y", "x", "c"), split_axis=0, concat_axis=0, tiled=True
    )
    copies = call(fold_kernel, [VMEM], [((32, 8, SEGLEN), f32)], "fold")(spread)
    spread_planes = [[4 * z + y for z in (0, 4, 2, 6, 1, 5, 3, 7) for y in range(4)]]
    sums = lax.all_to_all(
        copies, ("z", "y"), split_axis=0, concat_axis=0, axis_index_groups=spread_planes, tiled=True
    )
    return jnp.sum(sums.reshape(8, 32, SEGLEN), axis=0)


def solution(mesh):
    whole = Mesh(mesh.devices.reshape(8, 4, 4, 2), ALL)
    return jax.shard_map(
        local,
        mesh=whole,
        in_specs=(P(ALL, None), P(ALL), P(ALL), P(ALL), P(), P(), P(), P()),
        out_specs=P(("x", "c"), None),
        check_vma=False,
    )
```
